768 devices in a mesh: slab: 64 (over z_hi, y, core), grp: 12 (over x, z_lo).
Axes of the slice: x: 4, y: 8, z: 12 (z_hi: 4, z_lo: 3; z = z_hi * 3 + z_lo), core: 2. Of those that a mesh axis runs over, the one named last changes fastest.
Arguments:
- initial_samples: bfloat16 [48, 128, 4, 12288], P('grp', 'slab'), may hold values from -6 to 6
- courant_east: float32 [128, 2, 12288], P('slab'), may hold values from -0.45 to 0.45
- northward_courant: float32 [128, 2, 12288], P('slab'), may hold values from -0.45 to 0.45
- diffusivity: float32 [8, 4], replicated, may hold values from 0.02 to 0.2
- profile_index: int32 [128], P('slab'), may hold values from 0 to 7
- observations: float32 [128, 4, 12288], P(None, None, ('slab', 'grp')), may hold values from -6 to 6
- error_precision: float32 [4], replicated, may hold values from 0.3 to 3
- localization: float32 [4, 256], replicated, may hold values from 0.05 to 1
- patch_tiles: int32 [8, 768], P(None, ('slab', 'grp')), may hold values from 0 to 3
- patch_counts: int32 [8, 768], P(None, ('slab', 'grp')), may hold values from 16 to 256, as said below
Outputs:
- analysis_state: bfloat16 [48, 128, 4, 12288], P('grp', 'slab')
The draws below stay inside these ranges and needn't reach their ends.
Inputs may be any that keep to these rules, and one draw needn't show every extreme that they name: A patch observes its first patch_counts columns in row-major order; some patch observes all 256 columns and some exactly 16.
All inputs are finite; a program needn't handle non-finite values.
Results may differ from the reference program's by a relative error of at most 0.0052.
Values may be sent and summed in bfloat16 or wider, within the bound.
A program may use at most 64 MiB of HBM per device.

```python
import math
import jax
import jax.numpy as jnp
from jax import lax

LEVELS = 2
FIELDS = 2
VARS = 4
PATCH = 16
NS_ITERS = 4
NPROF = 8
TILES = 4
MEMBERS = 48
LAT = 128
LON = 12288


def draw_patch_counts(key, part):
    key = jax.random.fold_in(key, 11)
    counts = jax.random.randint(key, (LAT // PATCH, LON // PATCH), PATCH, PATCH * PATCH + 1)
    counts = counts.at[0, 0].set(PATCH * PATCH)
    counts = counts.at[-1, -1].set(PATCH)
    return counts.astype(jnp.int32)


def touch_ends(drawn, rng, least, high):
    longest = drawn.shape.index(max(drawn.shape))
    spots = []
    for shift in (0, 1):
        where = [jax.random.randint(jax.random.fold_in(rng, axis), (), 0, length) for axis, length in enumerate(drawn.shape)]
        where[longest] = (where[longest] + shift) % drawn.shape[longest]
        spots.append(tuple(where))
    return drawn.at[spots[0]].set(least).at[spots[1]].set(high)


def block_scale(stream_key, dims, split, smallest, high):
    loudness = 1.0
    for dim, blocks in split:
        steps = jax.random.uniform(jax.random.fold_in(jax.random.fold_in(stream_key, 6), dim), (blocks,), jnp.float32, smallest / len(split), high / len(split))
        loudness = loudness * jnp.repeat(jnp.exp(steps), dims[dim] // blocks).reshape((-1,) + (1,) * (len(dims) - 1 - dim))
    return loudness


def noise(key, extent, spread, bound, split=(), kind=jnp.bfloat16):
    loudness = block_scale(key, extent, split, -0.22, 0.18) if split else 1.0
    drawn = jax.random.normal(key, extent, jnp.float32) * spread * loudness
    return jnp.minimum(jnp.maximum(drawn, -bound), bound).astype(kind)


def setup_inputs(seed: int = 0) -> dict:
    splits = jax.random.split(jax.random.key(seed), 11)
    initial_samples = noise(splits[0], (MEMBERS, LAT, VARS, LON), 1.0, 6.0, ((0, 12), (1, 64)))
    courant_east = jnp.clip(jax.random.uniform(splits[1], (LAT, LEVELS, LON), jnp.float32, -0.45, 0.45) * block_scale(splits[1], (LAT, LEVELS, LON), ((0, 64),), -0.4, 0.0), -0.45, 0.45)
    northward_courant = jnp.clip(jax.random.uniform(splits[2], (LAT, LEVELS, LON), jnp.float32, -0.45, 0.45) * block_scale(splits[2], (LAT, LEVELS, LON), ((0, 64),), -0.4, 0.0), -0.45, 0.45)
    diffusivity = jnp.clip(jnp.exp(jax.random.uniform(splits[3], (NPROF, VARS), jnp.float32, math.log(0.02), math.log(0.2))), 0.02, 0.2)
    profile_index = touch_ends(jax.random.randint(splits[4], (LAT,), 0, NPROF), jax.random.fold_in(splits[4], 1), 0, NPROF - 1).astype(jnp.int32)
    observations = noise(splits[5], (LAT, VARS, LON), 1.0, 6.0, ((2, 768),), jnp.float32)
    error_precision = jnp.clip(jnp.exp(jax.random.uniform(splits[6], (VARS,), jnp.float32, math.log(0.3), math.log(3.0))), 0.3, 3.0)
    localization = jnp.clip(jnp.exp(jax.random.uniform(splits[7], (TILES, PATCH * PATCH), jnp.float32, math.log(0.05), math.log(1.0))), 0.05, 1.0)
    patch_tiles = touch_ends(jax.random.randint(splits[8], (LAT // PATCH, LON // PATCH), 0, TILES), jax.random.fold_in(splits[8], 1), 0, TILES - 1).astype(jnp.int32)
    patch_counts = draw_patch_counts(jax.random.fold_in(splits[10], 71), 0)
    return dict(initial_samples=initial_samples, courant_east=courant_east, northward_courant=northward_courant, diffusivity=diffusivity, profile_index=profile_index, observations=observations, error_precision=error_precision, localization=localization, patch_tiles=patch_tiles, patch_counts=patch_counts)


def advance(current, northern, southern, cour_east, cour_north, kappa):
    eastern = jnp.roll(current, -1, axis=-1)
    western = jnp.roll(current, 1, axis=-1)
    return current - 0.5 * cour_east * (eastern - western) - 0.5 * cour_north * (northern - southern) + kappa * (eastern + western + northern + southern - 4.0 * current)

def analyse(ensemble, observations, error_precision, localization, patch_tiles, patch_counts, patch_size, sweeps):
    members, lat_cells, var_count, longitude_cells = ensemble.shape
    row_count = lat_cells // patch_size
    col_count = longitude_cells // patch_size
    highest = lax.Precision.HIGHEST
    states = ensemble.astype(jnp.float32).reshape(members, row_count, patch_size, var_count, col_count, patch_size)
    average = lax.optimization_barrier(jnp.mean(states, axis=0))
    deviation = states - average
    position = jnp.arange(patch_size * patch_size, dtype=jnp.int32)
    observed = (position[None, None, :] < patch_counts[:, :, None]).astype(jnp.float32)
    tile_hot = (patch_tiles[:, :, None] == jnp.arange(localization.shape[0], dtype=jnp.int32)[None, None, :]).astype(jnp.float32)
    weights = jnp.einsum('rct,tq->rcq', tile_hot, localization, precision=highest) * observed
    weights = jnp.transpose(weights.reshape(row_count, col_count, patch_size, patch_size), (0, 2, 1, 3))
    precision_map = weights[:, :, None, :, :] * error_precision[None, None, :, None, None]
    weighted = deviation * precision_map
    gram_matrix = jnp.einsum('kryvcx,jryvcx->rckj', weighted, deviation, precision=highest)
    observation_misfit = observations.astype(jnp.float32).reshape(row_count, patch_size, var_count, col_count, patch_size) - average
    driving = jnp.einsum('kryvcx,ryvcx->rck', weighted, observation_misfit, precision=highest)
    identity = jnp.eye(members, dtype=jnp.float32)
    system = (members - 1.0) * identity + gram_matrix
    trace_sum = jnp.trace(system, axis1=2, axis2=3)
    scaled_iter = system / trace_sum[:, :, None, None]
    root_iter = jnp.broadcast_to(identity, system.shape)
    for sweep in range(sweeps):
        correction = 1.5 * identity - 0.5 * jnp.matmul(root_iter, scaled_iter, precision=highest)
        scaled_iter = jnp.matmul(scaled_iter, correction, precision=highest)
        root_iter = jnp.matmul(correction, root_iter, precision=highest)
    root_inverse = root_iter / jnp.sqrt(trace_sum)[:, :, None, None]
    mean_weights = jnp.matmul(root_inverse, jnp.matmul(root_inverse, driving[..., None], precision=highest), precision=highest)
    weights_all = math.sqrt(members - 1.0) * root_inverse + mean_weights
    analysis_increment = jnp.einsum('jryvcx,rcjk->kryvcx', deviation, weights_all, precision=highest)
    return (average + analysis_increment).reshape(members, lat_cells, var_count, longitude_cells).astype(jnp.bfloat16)

def reference(initial_samples, courant_east, northward_courant, diffusivity, profile_index, observations, error_precision, localization, patch_tiles, patch_counts):
    cour_east = jnp.repeat(courant_east, FIELDS, axis=1)
    cour_north = jnp.repeat(northward_courant, FIELDS, axis=1)
    kappa = diffusivity[profile_index][:, :, None]

    def predicted_field(sample_position):
        current = sample_position.astype(jnp.float32)
        for sweep in range(2):
            blank_line_vector = jnp.zeros_like(current[:1])
            northern = jnp.concatenate([current[1:], blank_line_vector], 0)
            southern = jnp.concatenate([blank_line_vector, current[:-1]], 0)
            current = advance(current, northern, southern, cour_east, cour_north, kappa)
        return current.astype(jnp.bfloat16)
    first_guess_average = lax.map(predicted_field, initial_samples)

    def analyse_row(row_index):
        start = row_index * PATCH
        block = lax.dynamic_slice_in_dim(first_guess_average, start, PATCH, 1)
        observed_rows = lax.dynamic_slice_in_dim(observations, start, PATCH, 0)
        tile_row = lax.dynamic_slice_in_dim(patch_tiles, row_index, 1, 0)
        count_row = lax.dynamic_slice_in_dim(patch_counts, row_index, 1, 0)
        return analyse(block, observed_rows, error_precision, localization, tile_row, count_row, PATCH, NS_ITERS)
    updated_estimate = lax.map(analyse_row, jnp.arange(LAT // PATCH, dtype=jnp.int32))
    return jnp.transpose(updated_estimate, (1, 0, 2, 3, 4)).reshape(MEMBERS, LAT, VARS, LON)
```

```python
import functools
import math

import jax
import jax.numpy as jnp
from jax import lax
from jax.experimental import pallas as pl
from jax.experimental.pallas import tpu as pltpu
from jax.sharding import PartitionSpec as P

PATCH = 16
NS_ITERS = 4
F32 = jnp.float32
BF16 = jnp.bfloat16
VMEM_LIMIT = 56 * 1024 * 1024
LANES = 128
ROWS = 8
PAD = 64


def lane_ids(rows):
    return lax.broadcasted_iota(jnp.int32, (rows, LANES), 1)


def pack_kernel(groups, prof_ref, diff_ref, x_ref, ce_ref, cn_ref, s_ref, c_ref):
    blocks = ROWS * groups
    me = lax.axis_index("grp")
    lane4 = lane_ids(4)

    def tiles(b):
        at = pl.ds(pl.multiple_of(b * LANES, LANES), LANES)
        return [[x_ref[m, r, :, at].astype(F32) for r in range(2)] for m in range(4)]

    def turned(x, r, v):
        return jnp.concatenate([x[m][r][v : v + 1] for m in range(4)], axis=0)

    def one(b, carry):
        x = tiles(b)
        for r in range(2):
            for v in range(4):
                s_ref[b, r * 4 + v] = turned(x, r, v).astype(BF16)
        return carry

    lax.fori_loop(0, blocks, one, 0)

    def edges(b, carry):
        before = lax.rem(b + blocks - 1, blocks)
        after = lax.rem(b + 1, blocks)
        packed = jnp.zeros((4, LANES), F32)
        for k in range(8):
            mixed = jnp.where(lane4 < 64, s_ref[after, k].astype(F32), s_ref[before, k].astype(F32))
            moved = pltpu.roll(mixed, 2 + 8 * k, 1)
            packed = jnp.where((lane4 >= 8 * k) & (lane4 < 8 * k + 4), moved, packed)
        s_ref[b, 8] = packed.astype(BF16)
        return carry

    lax.fori_loop(0, blocks, edges, 0)

    kappas = []
    for r in range(2):
        for v in range(4):
            kappas.append(jnp.full((1, LANES), diff_ref[prof_ref[r], v], F32))
    kappa = jnp.concatenate(kappas, axis=0)
    lane1 = lane_ids(1)
    kappa_lanes = jnp.zeros((1, LANES), F32)
    for k in range(8):
        kappa_lanes = jnp.where(lane1 // 8 == k, kappas[k], kappa_lanes)

    lane8 = lane_ids(8)
    sub8 = lax.broadcasted_iota(jnp.int32, (8, LANES), 0)
    mine = (lax.rem(sub8, 4) == lane8 // 16) & (lane8 < 64)

    def courant(b):
        at = pl.ds(pl.multiple_of(b * LANES, LANES), LANES)
        return jnp.concatenate([ce_ref[0, :, at], ce_ref[1, :, at], cn_ref[0, :, at], cn_ref[1, :, at]], axis=0)

    for i in range(ROWS):
        b = me * ROWS + i
        here = courant(b)
        before = courant(lax.rem(b + blocks - 1, blocks))
        after = courant(lax.rem(b + 1, blocks))
        low = jnp.broadcast_to(before[:, LANES - 1 : LANES], (8, LANES))
        high = jnp.broadcast_to(after[:, 0:1], (8, LANES))
        side = jnp.where(mine, jnp.where(lax.rem(lane8, 8) == 1, low, high), 0.0)
        c_ref[i, 0:8] = here
        c_ref[i, 8:16] = jnp.concatenate(
            [
                jnp.sum(side[0:4], axis=0, keepdims=True),
                jnp.sum(side[4:8], axis=0, keepdims=True),
                kappa_lanes,
                jnp.zeros((5, LANES), F32),
            ],
            axis=0,
        )
        c_ref[i, 16:24] = kappa


def analysis_kernel(
    groups, slabs, ep_ref, r_ref, low_ref, high_ref, c_ref, low_c_ref, high_c_ref, rm_ref,
    y_ref, x0, hx, hs, x1, bg, dev, wts, rc_ref
):
    members = 4 * groups
    slab = lax.axis_index("slab")
    row = slab // ROWS
    has_low = row > 0
    has_high = row < slabs // ROWS - 1
    lane = lane_ids(members)
    lane1 = lane_ids(1)

    rc_ref[0] = low_c_ref[...]
    rc_ref[9] = high_c_ref[...]
    for s in range(8):
        rc_ref[s + 1] = c_ref[s]

    def coefs(s, ce, cn, kappa):
        east = kappa - 0.5 * ce
        west = kappa + 0.5 * ce
        north = kappa - 0.5 * cn
        south = kappa + 0.5 * cn
        return 1.0 - 4.0 * kappa, east, west, north, south

    def outside(s):
        return ((s == 0) & jnp.logical_not(has_low)) | ((s == 9) & jnp.logical_not(has_high))

    def load(s, read, gone):
        def whole(k):
            x = read(k).astype(F32).reshape(members, LANES)
            return x if gone is None else jnp.where(gone, 0.0, x)

        edge = whole(8)
        for k in range(8):
            x = whole(k)
            x0[s * 8 + k] = x
            own = pltpu.roll(x, 8 * k + 5, 1)
            edge = jnp.where((lane == 8 * k + 4) | (lane == 8 * k + 5), own, edge)
        hs[s] = edge

    def load_own(s, carry):
        load(s, lambda k: r_ref[:, s - 1, k], None)
        return carry

    load(0, lambda k: low_ref[:, k], jnp.logical_not(has_low))
    lax.fori_loop(1, 9, load_own, 0)
    load(9, lambda k: high_ref[:, k], jnp.logical_not(has_high))
    half = lane < 64
    packed = [jnp.where(half, hs[2 * q], pltpu.roll(hs[2 * q + 1], 64, 1)) for q in range(5)]

    def pair(a, b):
        return jnp.where(lane1 < 64, a, pltpu.roll(b, 64, 1))

    def swap(x):
        return jnp.where(lax.rem(lane, 8) == 1, pltpu.roll(x, LANES - 1, 1), pltpu.roll(x, 1, 1))

    for q in range(5):
        hx[q] = swap(packed[q])
    stepped = []
    for q in range(5):
        x = packed[q]
        nxt = packed[min(q + 1, 4)]
        prv = packed[max(q - 1, 0)]
        north = jnp.where(lane < 96, pltpu.roll(x, 96, 1), pltpu.roll(nxt, 96, 1))
        south = jnp.where(lane >= 32, pltpu.roll(x, 32, 1), pltpu.roll(prv, 32, 1))
        low = lax.rem(lane, 8) == 1
        east = jnp.where(low, pltpu.roll(x, LANES - 4, 1), pltpu.roll(x, LANES - 1, 1))
        west = jnp.where(low, pltpu.roll(x, 1, 1), pltpu.roll(x, LANES - 2, 1))
        both = [pair(rc_ref[2 * q, 8 + n : 9 + n], rc_ref[2 * q + 1, 8 + n : 9 + n]) for n in range(3)]
        cc, ke, kw, kn, ks = coefs(0, *both)
        new = x * cc + east * ke + west * kw + north * kn + south * ks
        if q == 0:
            new = jnp.where(half & jnp.logical_not(has_low), 0.0, new)
        if q == 4:
            new = jnp.where(jnp.logical_not(half) & jnp.logical_not(has_high), 0.0, new)
        stepped.append(new)
    for q in range(5):
        hx[5 + q] = swap(stepped[q])

    def advance(src, edge_at, t, s, r, v, offset):
        x = src[t - offset * 4]
        north = src[t + 4 - offset * 4]
        south = src[t - 4 - offset * 4]
        base = lax.rem(t, 16) * 8
        edge = pltpu.roll(hx[edge_at + t // 16], lax.rem(254 - base, LANES), 1)
        west = jnp.where(lane == 0, edge, pltpu.roll(x, 1, 1))
        east = jnp.where(lane == LANES - 1, edge, pltpu.roll(x, LANES - 1, 1))
        ce = rc_ref[s, pl.ds(2 * r + v // 2, 1)]
        cn = rc_ref[s, pl.ds(4 + 2 * r + v // 2, 1)]
        kappa = rc_ref[s, pl.ds(16 + 4 * r + v, 1)]
        cc, ke, kw, kn, ks = coefs(0, ce, cn, kappa)
        return x * cc + east * ke + west * kw + north * kn + south * ks

    def first(n, carry):
        s = n // 2
        r = lax.rem(n, 2)
        gone = outside(s)
        for v in range(4):
            new = advance(x0, 0, n * 4 + v, s, r, v, 0)
            x1[n * 4 + v - 4] = jnp.where(gone, 0.0, new)
        return carry

    lax.fori_loop(1, 19, first, 0)

    lane8 = lane_ids(8)
    obs = []
    for a in range(8):
        tile = jnp.zeros((8, LANES), F32)
        for q in range(8):
            tile = jnp.where(lane8 // 16 == q, pltpu.roll(rm_ref[q, 0], (16 * (q - a)) % LANES, 1), tile)
        obs.append(tile)
    root_w = []
    for h in range(2):
        tile = jnp.zeros((8, LANES), F32)
        for q in range(8):
            tile = jnp.where(lane8 // 16 == q, pltpu.roll(rm_ref[q, 1], (16 * (q - h)) % LANES, 1), tile)
        root_w.append(tile)

    spare = jnp.zeros((PAD - members - 1, LANES), BF16)
    for c in range(8):
        for r in range(2):
            rho = 2 * c + r
            for v in range(4):
                t = (rho + 2) * 4 + v
                new = advance(x1, 5, t, c + 1, r, v, 1)
                rounded = new.astype(BF16)
                back = rounded.astype(F32)
                k = r * 4 + v
                at = slice(k * LANES, (k + 1) * LANES)
                bg[c, :, at] = rounded
                average = jnp.sum(back, axis=0, keepdims=True) * (1.0 / members)
                scale = root_w[rho // 8][rho % 8 : rho % 8 + 1] * ep_ref[v]
                tt = rho * 4 + v
                misfit = (obs[tt // 8][tt % 8 : tt % 8 + 1] - average) * scale
                dev[c, 0:members, at] = ((back - average) * scale).astype(BF16)
                dev[c, members:PAD, at] = jnp.concatenate(
                    [misfit, jnp.zeros((PAD - members - 1, LANES), F32)], axis=0
                ).astype(BF16)

    wide = lax.broadcasted_iota(jnp.int32, (PAD, 8 * LANES), 1)
    strip_of = lax.rem(wide, LANES) // 16

    def gram(c, acc):
        a = dev[c]
        zero = jnp.zeros_like(a)
        stack = jnp.concatenate([jnp.where(strip_of == p, a, zero) for p in range(8)], axis=0)
        return acc + lax.dot_general(stack, a, (((1,), (1,)), ((), ())), preferred_element_type=F32)

    grams = lax.fori_loop(0, 8, gram, jnp.zeros((8 * PAD, PAD), F32))

    si = lax.broadcasted_iota(jnp.int32, (PAD, PAD), 0)
    li = lax.broadcasted_iota(jnp.int32, (PAD, PAD), 1)
    inside = (si < members) & (li < members)
    eye = jnp.where((si == li) & inside, 1.0, 0.0)
    dot = functools.partial(jnp.dot, preferred_element_type=F32, precision=lax.Precision.HIGHEST)
    zs, ys, traces = [], [], []
    for p in range(8):
        full = grams[p * PAD : (p + 1) * PAD]
        system = jnp.where(inside, full, 0.0) + (members - 1.0) * eye
        trace = jnp.sum(jnp.sum(system * eye, axis=1, keepdims=True), axis=0, keepdims=True)
        traces.append(trace)
        ys.append(system / trace)
        zs.append(eye)
    for sweep in range(NS_ITERS):
        cs = []
        for p in range(8):
            zy = ys[p] if sweep == 0 else dot(zs[p], ys[p])
            cs.append(1.5 * eye - 0.5 * zy)
        for p in range(8):
            if sweep < NS_ITERS - 1:
                ys[p] = dot(ys[p], cs[p])
            zs[p] = cs[p] if sweep == 0 else dot(cs[p], zs[p])
    heads, tails = [], []
    for p in range(8):
        full = grams[p * PAD : (p + 1) * PAD]
        root = zs[p] / jnp.sqrt(traces[p])
        drive = jnp.where(li[0:1] < members, full[members : members + 1], 0.0)
        first_col = jnp.sum(root * drive, axis=1, keepdims=True)
        mean_row = jnp.sum(root * first_col, axis=0, keepdims=True)
        w = math.sqrt(members - 1.0) * root + mean_row
        total = jnp.sum(w, axis=1, keepdims=True)
        w = jnp.where(inside, w + (1.0 - total) * (1.0 / members), 0.0)[0:members]
        head = w.astype(BF16)
        heads.append(head.astype(F32))
        tails.append(w - head.astype(F32))
    wts[0:members] = jnp.concatenate(heads, axis=1).astype(BF16)
    wts[members : 2 * members] = jnp.concatenate(tails, axis=1).astype(BF16)

    wide2 = lax.broadcasted_iota(jnp.int32, (members, 2 * LANES), 1)
    strip2 = lax.rem(wide2, LANES) // 16
    fill = jnp.zeros((PAD - members, 2 * LANES), BF16)

    def combine(c, carry):
        for pair_at in range(4):
            b = bg[c, :, pair_at * 2 * LANES : (pair_at + 1) * 2 * LANES]
            zero = jnp.zeros_like(b)
            parts = []
            for p in range(8):
                parts += [jnp.where(strip2 == p, b, zero), fill]
            stack = jnp.concatenate(parts, axis=0)
            out = jnp.dot(wts[...], stack, preferred_element_type=F32)
            out = out[0:members] + out[members : 2 * members]
            for k in range(2):
                y_ref[:, c, pair_at * 2 + k] = (
                    out[:, k * LANES : (k + 1) * LANES].reshape(groups, 4, LANES).astype(BF16)
                )
        return carry

    lax.fori_loop(0, 8, combine, 0)


def unpack_kernel(o_ref, out_ref):
    def one(b, carry):
        at = pl.ds(pl.multiple_of(b * LANES, LANES), LANES)
        for r in range(2):
            x = [o_ref[b, r * 4 + v].astype(F32) for v in range(4)]
            for m in range(4):
                out_ref[m, r, :, at] = jnp.concatenate(
                    [x[v][m : m + 1] for v in range(4)], axis=0
                ).astype(BF16)
        return carry

    lax.fori_loop(0, o_ref.shape[0], one, 0)


def on_device(
    initial_samples,
    courant_east,
    northward_courant,
    diffusivity,
    profile_index,
    observations,
    error_precision,
    localization,
    patch_tiles,
    patch_counts,
):
    slabs = lax.axis_size("slab")
    groups = lax.axis_size("grp")
    blocks = ROWS * groups
    rows = slabs // ROWS
    members = 4 * groups
    vmem = pl.BlockSpec(memory_space=pltpu.VMEM)
    smem = pl.BlockSpec(memory_space=pltpu.SMEM)
    params = pltpu.CompilerParams(vmem_limit_bytes=VMEM_LIMIT)

    sent, courants = pl.pallas_call(
        functools.partial(pack_kernel, groups),
        out_shape=(
            jax.ShapeDtypeStruct((blocks, 9, 4, LANES), BF16),
            jax.ShapeDtypeStruct((ROWS, 24, LANES), F32),
        ),
        in_specs=[smem, smem, vmem, vmem, vmem],
        out_specs=(vmem, vmem),
        compiler_params=params,
        name="pack",
    )(profile_index, diffusivity, initial_samples, courant_east, northward_courant)

    obs = observations.reshape(rows, 8, 8, 16).transpose(0, 2, 1, 3).reshape(rows, 8, LANES)
    tile_hot = patch_tiles == jnp.arange(localization.shape[0], dtype=jnp.int32)[None]
    weight = jnp.sum(jnp.where(tile_hot[:, :, None], localization[None], 0.0), axis=1)
    weight = jnp.where(jnp.arange(PATCH * PATCH, dtype=jnp.int32)[None] < patch_counts, weight, 0.0)
    root = jnp.sqrt(weight).reshape(rows, 2, 8, 16).transpose(0, 2, 1, 3).reshape(rows, 8, 32)
    root = jnp.pad(root, ((0, 0), (0, 0), (0, LANES - 32)))
    notes = jnp.stack([obs, root], axis=1)

    both = ("slab", "grp")
    near = [[(r * ROWS + i) * groups + g for g in range(groups) for i in range(ROWS)] for r in range(rows)]
    slab_near = [[r * ROWS + i for i in range(ROWS)] for r in range(rows)]
    slab_far = [[r * ROWS + i for r in range(rows)] for i in range(ROWS)]
    rise = [(s, s + ROWS) for s in range(slabs - ROWS)]
    fall = [(s + ROWS, s) for s in range(slabs - ROWS)]

    home_of = [
        (f, ((f % 8) * ROWS + (f // 8) % ROWS) * groups + f // (8 * ROWS)) for f in range(slabs * groups)
    ]
    notes = lax.ppermute(notes, both, home_of)
    got_m = lax.all_to_all(notes, "slab", 0, 0, axis_index_groups=slab_far, tiled=True)
    got_c = lax.all_to_all(courants, "slab", 0, 0, axis_index_groups=slab_near, tiled=True)
    low_c = lax.ppermute(got_c[ROWS - 1], "slab", rise)
    high_c = lax.ppermute(got_c[0], "slab", fall)
    got = lax.all_to_all(sent, both, 0, 0, axis_index_groups=near, tiled=True)
    got = got.reshape(groups, ROWS, 9, 4, LANES)
    low = lax.ppermute(got[:, ROWS - 1], "slab", rise)
    high = lax.ppermute(got[:, 0], "slab", fall)

    analysed = pl.pallas_call(
        functools.partial(analysis_kernel, groups, slabs),
        out_shape=jax.ShapeDtypeStruct((groups, ROWS, 8, 4, LANES), BF16),
        in_specs=[smem] + [vmem] * 7,
        out_specs=vmem,
        scratch_shapes=[
            pltpu.VMEM((80, members, LANES), F32),
            pltpu.VMEM((10, members, LANES), F32),
            pltpu.VMEM((10, members, LANES), F32),
            pltpu.VMEM((72, members, LANES), F32),
            pltpu.VMEM((8, members, 8 * LANES), BF16),
            pltpu.VMEM((8, PAD, 8 * LANES), BF16),
            pltpu.VMEM((2 * members, 8 * PAD), BF16),
            pltpu.VMEM((10, 24, LANES), F32),
        ],
        compiler_params=params,
        name="analysis",
    )(jnp.sqrt(error_precision), got, low, high, got_c, low_c, high_c, got_m)

    home = lax.all_to_all(
        analysed.reshape(blocks, 8, 4, LANES), both, 0, 0, axis_index_groups=near, tiled=True
    )

    return pl.pallas_call(
        unpack_kernel,
        out_shape=jax.ShapeDtypeStruct((4, 2, 4, blocks * LANES), BF16),
        in_specs=[vmem],
        out_specs=vmem,
        compiler_params=params,
        name="unpack",
    )(home)


def solution(mesh):
    return jax.shard_map(
        on_device,
        mesh=mesh,
        in_specs=(
            P("grp", "slab", None, None),
            P("slab", None, None),
            P("slab", None, None),
            P(),
            P("slab"),
            P(None, None, ("slab", "grp")),
            P(),
            P(),
            P(None, ("slab", "grp")),
            P(None, ("slab", "grp")),
        ),
        out_specs=P("grp", "slab", None, None),
        check_vma=False,
    )
```

```python
import functools
import math

import jax
import jax.numpy as jnp
from jax import lax
from jax.experimental import pallas as pl
from jax.experimental.pallas import tpu as pltpu
from jax.sharding import PartitionSpec as P

PATCH = 16
NS_ITERS = 4
F32 = jnp.float32
BF16 = jnp.bfloat16
VMEM_LIMIT = 56 * 1024 * 1024
LANES = 128
ROWS = 8
PAD = 64


def lane_ids(rows):
    return lax.broadcasted_iota(jnp.int32, (rows, LANES), 1)


def pack_kernel(groups, prof_ref, diff_ref, x_ref, ce_ref, cn_ref, s_ref):
    blocks = ROWS * groups
    me = lax.axis_index("grp")
    part = lax.rem(me // 4, 3)
    kind = lax.rem(me, 4)
    lane4 = lane_ids(4)

    def place(b):
        return pl.ds(pl.multiple_of(b * LANES, LANES), LANES)

    def one(b, carry):
        at = place(b)
        for r in range(2):
            x = [x_ref[m, r, :, at].astype(F32) for m in range(4)]
            for v in range(4):
                s_ref[b, r * 4 + v] = jnp.concatenate([x[m][v : v + 1] for m in range(4)], axis=0).astype(BF16)
        return carry

    lax.fori_loop(0, blocks, one, 0, unroll=4)

    def edges(b, carry):
        before = lax.rem(b + blocks - 1, blocks)
        after = lax.rem(b + 1, blocks)
        packed = jnp.zeros((4, LANES), F32)
        for k in range(8):
            mixed = jnp.where(lane4 < 64, s_ref[after, k].astype(F32), s_ref[before, k].astype(F32))
            moved = pltpu.roll(mixed, 2 + 8 * k, 1)
            packed = jnp.where((lane4 >= 8 * k) & (lane4 < 8 * k + 4), moved, packed)
        s_ref[b, 8] = packed.astype(BF16)
        return carry

    lax.fori_loop(0, blocks, edges, 0, unroll=4)

    def term(x):
        high = x.astype(BF16).astype(F32)
        rest = x - high
        middle = rest.astype(BF16).astype(F32)
        return jnp.where(part == 0, high, jnp.where(part == 1, middle, rest - middle)).astype(BF16)

    def whole(ref, at):
        return jnp.concatenate([ref[0, :, at], ref[1, :, at]], axis=0)

    def plain(ref):
        def go(b, carry):
            s_ref[b, 9] = term(whole(ref, place(b)))
            return carry

        lax.fori_loop(0, blocks, go, 0, unroll=4)

    @pl.when(kind == 0)
    def _():
        plain(ce_ref)

    @pl.when(kind == 1)
    def _():
        plain(cn_ref)

    @pl.when(kind == 2)
    def _():
        lane1 = lane_ids(1)
        kappa_lanes = jnp.zeros((1, LANES), F32)
        for k in range(8):
            value = diff_ref[prof_ref[k // 4], k % 4]
            kappa_lanes = jnp.where(lane1 // 8 == k, value, kappa_lanes)
        sub4 = lax.broadcasted_iota(jnp.int32, (4, LANES), 0)
        mine = (sub4 == lane4 // 16) & (lane4 < 64)
        low_at = lax.rem(lane4, 8) == 1

        def go(b, carry):
            before = place(lax.rem(b + blocks - 1, blocks))
            after = place(lax.rem(b + 1, blocks))
            rows = []
            for ref in (ce_ref, cn_ref):
                low = jnp.broadcast_to(whole(ref, before)[:, LANES - 1 : LANES], (4, LANES))
                high = jnp.broadcast_to(whole(ref, after)[:, 0:1], (4, LANES))
                side = jnp.where(mine, jnp.where(low_at, low, high), 0.0)
                rows.append(jnp.sum(side, axis=0, keepdims=True))
            s_ref[b, 9] = term(jnp.concatenate(rows + [kappa_lanes, jnp.zeros((1, LANES), F32)], axis=0))
            return carry

        lax.fori_loop(0, blocks, go, 0, unroll=4)

    @pl.when(kind == 3)
    def _():
        def go(b, carry):
            s_ref[b, 9] = jnp.zeros((4, LANES), BF16)
            return carry

        lax.fori_loop(0, blocks, go, 0, unroll=4)


def spread_kernel(n_ref, o_ref):
    q = lax.axis_index("slab") // ROWS
    lane = lane_ids(8)
    mine = lane // 16 == q

    def go(row, carry):
        for a in range(10):
            k = a // 8
            shift = lax.rem(16 * (q + 8 - a % 8), LANES)
            o_ref[row, a] = jnp.where(mine, pltpu.roll(n_ref[row, k], shift, 1), 0.0)
        return carry

    lax.fori_loop(0, n_ref.shape[0], go, 0)


def analysis_kernel(
    groups, slabs, ep_ref, r_ref, low_ref, high_ref, rm_ref,
    y_ref, x0, hx, hs, x1, bg, dev, wts, rc_ref
):
    members = 4 * groups
    slab = lax.axis_index("slab")
    row = slab // ROWS
    has_low = row > 0
    has_high = row < slabs // ROWS - 1
    lane = lane_ids(members)
    lane1 = lane_ids(1)


    def coefs(s, ce, cn, kappa):
        east = kappa - 0.5 * ce
        west = kappa + 0.5 * ce
        north = kappa - 0.5 * cn
        south = kappa + 0.5 * cn
        return 1.0 - 4.0 * kappa, east, west, north, south

    def outside(s):
        return ((s == 0) & jnp.logical_not(has_low)) | ((s == 9) & jnp.logical_not(has_high))

    def load(s, read, gone):
        def whole(k):
            x = read(k).astype(F32).reshape(members, LANES)
            return x if gone is None else jnp.where(gone, 0.0, x)

        edge = whole(8)
        for k in range(8):
            x = whole(k)
            x0[s * 8 + k] = x
            own = pltpu.roll(x, 8 * k + 5, 1)
            edge = jnp.where((lane == 8 * k + 4) | (lane == 8 * k + 5), own, edge)
        hs[s] = edge
        rows = whole(9)
        rows = rows[0:16] + rows[16:32] + rows[32:48]
        rc_ref[s, 0:16] = rows
        rc_ref[s, 16:24] = jnp.concatenate(
            [jnp.broadcast_to(rows[10:11, 8 * k : 8 * k + 1], (1, LANES)) for k in range(8)], axis=0
        )

    def load_own(s, carry):
        load(s, lambda k: r_ref[:, s - 1, k], None)
        return carry

    load(0, lambda k: low_ref[:, k], jnp.logical_not(has_low))
    lax.fori_loop(1, 9, load_own, 0, unroll=2)
    load(9, lambda k: high_ref[:, k], jnp.logical_not(has_high))
    half = lane < 64
    packed = [jnp.where(half, hs[2 * q], pltpu.roll(hs[2 * q + 1], 64, 1)) for q in range(5)]

    def pair(a, b):
        return jnp.where(lane1 < 64, a, pltpu.roll(b, 64, 1))

    def swap(x):
        return jnp.where(lax.rem(lane, 8) == 1, pltpu.roll(x, LANES - 1, 1), pltpu.roll(x, 1, 1))

    for q in range(5):
        hx[q] = swap(packed[q])
    stepped = []
    for q in range(5):
        x = packed[q]
        nxt = packed[min(q + 1, 4)]
        prv = packed[max(q - 1, 0)]
        north = jnp.where(lane < 96, pltpu.roll(x, 96, 1), pltpu.roll(nxt, 96, 1))
        south = jnp.where(lane >= 32, pltpu.roll(x, 32, 1), pltpu.roll(prv, 32, 1))
        low = lax.rem(lane, 8) == 1
        east = jnp.where(low, pltpu.roll(x, LANES - 4, 1), pltpu.roll(x, LANES - 1, 1))
        west = jnp.where(low, pltpu.roll(x, 1, 1), pltpu.roll(x, LANES - 2, 1))
        both = [pair(rc_ref[2 * q, 8 + n : 9 + n], rc_ref[2 * q + 1, 8 + n : 9 + n]) for n in range(3)]
        cc, ke, kw, kn, ks = coefs(0, *both)
        new = x * cc + east * ke + west * kw + north * kn + south * ks
        if q == 0:
            new = jnp.where(half & jnp.logical_not(has_low), 0.0, new)
        if q == 4:
            new = jnp.where(jnp.logical_not(half) & jnp.logical_not(has_high), 0.0, new)
        stepped.append(new)
    for q in range(5):
        hx[5 + q] = swap(stepped[q])

    def advance(src, edge_at, t, s, r, v, offset):
        x = src[t - offset * 4]
        north = src[t + 4 - offset * 4]
        south = src[t - 4 - offset * 4]
        base = lax.rem(t, 16) * 8
        edge = pltpu.roll(hx[edge_at + t // 16], lax.rem(254 - base, LANES), 1)
        west = jnp.where(lane == 0, edge, pltpu.roll(x, 1, 1))
        east = jnp.where(lane == LANES - 1, edge, pltpu.roll(x, LANES - 1, 1))
        ce = rc_ref[s, pl.ds(2 * r + v // 2, 1)]
        cn = rc_ref[s, pl.ds(4 + 2 * r + v // 2, 1)]
        kappa = rc_ref[s, pl.ds(16 + 4 * r + v, 1)]
        cc, ke, kw, kn, ks = coefs(0, ce, cn, kappa)
        return x * cc + east * ke + west * kw + north * kn + south * ks

    def first(n, carry):
        s = n // 2
        r = lax.rem(n, 2)
        gone = outside(s)
        for v in range(4):
            new = advance(x0, 0, n * 4 + v, s, r, v, 0)
            x1[n * 4 + v - 4] = jnp.where(gone, 0.0, new)
        return carry

    lax.fori_loop(1, 19, first, 0, unroll=2)

    obs = [rm_ref[a] for a in range(8)]
    root_w = [rm_ref[8 + h] for h in range(2)]

    for c in range(8):
        for r in range(2):
            rho = 2 * c + r
            for v in range(4):
                t = (rho + 2) * 4 + v
                new = advance(x1, 5, t, c + 1, r, v, 1)
                rounded = new.astype(BF16)
                back = rounded.astype(F32)
                k = r * 4 + v
                at = slice(k * LANES, (k + 1) * LANES)
                bg[c, :, at] = rounded
                average = jnp.sum(back, axis=0, keepdims=True) * (1.0 / members)
                scale = root_w[rho // 8][rho % 8 : rho % 8 + 1] * ep_ref[v]
                tt = rho * 4 + v
                misfit = (obs[tt // 8][tt % 8 : tt % 8 + 1] - average) * scale
                dev[c, 0:members, at] = ((back - average) * scale).astype(BF16)
                dev[c, members:PAD, at] = jnp.concatenate(
                    [misfit, jnp.zeros((PAD - members - 1, LANES), F32)], axis=0
                ).astype(BF16)

    wide = lax.broadcasted_iota(jnp.int32, (PAD, 8 * LANES), 1)
    strip_of = lax.rem(wide, LANES) // 16

    def gram(c, acc):
        a = dev[c]
        zero = jnp.zeros_like(a)
        stack = jnp.concatenate([jnp.where(strip_of == p, a, zero) for p in range(8)], axis=0)
        return acc + lax.dot_general(stack, a, (((1,), (1,)), ((), ())), preferred_element_type=F32)

    grams = lax.fori_loop(0, 8, gram, jnp.zeros((8 * PAD, PAD), F32))

    si = lax.broadcasted_iota(jnp.int32, (PAD, PAD), 0)
    li = lax.broadcasted_iota(jnp.int32, (PAD, PAD), 1)
    inside = (si < members) & (li < members)
    eye = jnp.where((si == li) & inside, 1.0, 0.0)
    dot = functools.partial(jnp.dot, preferred_element_type=F32, precision=lax.Precision.HIGHEST)
    zs, ys, traces = [], [], []
    for p in range(8):
        full = grams[p * PAD : (p + 1) * PAD]
        system = jnp.where(inside, full, 0.0) + (members - 1.0) * eye
        trace = jnp.sum(jnp.sum(system * eye, axis=1, keepdims=True), axis=0, keepdims=True)
        traces.append(trace)
        ys.append(system / trace)
        zs.append(eye)
    for sweep in range(NS_ITERS):
        cs = []
        for p in range(8):
            zy = ys[p] if sweep == 0 else dot(zs[p], ys[p])
            cs.append(1.5 * eye - 0.5 * zy)
        for p in range(8):
            if sweep < NS_ITERS - 1:
                ys[p] = dot(ys[p], cs[p])
            zs[p] = cs[p] if sweep == 0 else dot(cs[p], zs[p])
    heads, tails = [], []
    for p in range(8):
        full = grams[p * PAD : (p + 1) * PAD]
        root = zs[p] / jnp.sqrt(traces[p])
        drive = jnp.where(li[0:1] < members, full[members : members + 1], 0.0)
        first_col = jnp.sum(root * drive, axis=1, keepdims=True)
        mean_row = jnp.sum(root * first_col, axis=0, keepdims=True)
        w = math.sqrt(members - 1.0) * root + mean_row
        total = jnp.sum(w, axis=1, keepdims=True)
        w = jnp.where(inside, w + (1.0 - total) * (1.0 / members), 0.0)[0:members]
        head = w.astype(BF16)
        heads.append(head.astype(F32))
        tails.append(w - head.astype(F32))
    wts[0:members] = jnp.concatenate(heads, axis=1).astype(BF16)
    wts[members : 2 * members] = jnp.concatenate(tails, axis=1).astype(BF16)

    wide2 = lax.broadcasted_iota(jnp.int32, (members, 2 * LANES), 1)
    strip2 = lax.rem(wide2, LANES) // 16
    fill = jnp.zeros((PAD - members, 2 * LANES), BF16)

    def combine(c, carry):
        for pair_at in range(4):
            b = bg[c, :, pair_at * 2 * LANES : (pair_at + 1) * 2 * LANES]
            zero = jnp.zeros_like(b)
            parts = []
            for p in range(8):
                parts += [jnp.where(strip2 == p, b, zero), fill]
            stack = jnp.concatenate(parts, axis=0)
            out = jnp.dot(wts[...], stack, preferred_element_type=F32)
            out = out[0:members] + out[members : 2 * members]
            for k in range(2):
                y_ref[:, c, pair_at * 2 + k] = (
                    out[:, k * LANES : (k + 1) * LANES].reshape(groups, 4, LANES).astype(BF16)
                )
        return carry

    lax.fori_loop(0, 8, combine, 0)


def unpack_kernel(o_ref, out_ref):
    def one(b, carry):
        at = pl.ds(pl.multiple_of(b * LANES, LANES), LANES)
        for r in range(2):
            x = [o_ref[b, r * 4 + v].astype(F32) for v in range(4)]
            for m in range(4):
                out_ref[m, r, :, at] = jnp.concatenate(
                    [x[v][m : m + 1] for v in range(4)], axis=0
                ).astype(BF16)
        return carry

    lax.fori_loop(0, o_ref.shape[0], one, 0)


def on_device(
    initial_samples,
    courant_east,
    northward_courant,
    diffusivity,
    profile_index,
    observations,
    error_precision,
    localization,
    patch_tiles,
    patch_counts,
):
    slabs = lax.axis_size("slab")
    groups = lax.axis_size("grp")
    blocks = ROWS * groups
    rows = slabs // ROWS
    members = 4 * groups
    vmem = pl.BlockSpec(memory_space=pltpu.VMEM)
    smem = pl.BlockSpec(memory_space=pltpu.SMEM)
    params = pltpu.CompilerParams(vmem_limit_bytes=VMEM_LIMIT)

    sent = pl.pallas_call(
        functools.partial(pack_kernel, groups),
        out_shape=jax.ShapeDtypeStruct((blocks, 10, 4, LANES), BF16),
        in_specs=[smem, smem, vmem, vmem, vmem],
        out_specs=vmem,
        compiler_params=params,
        name="pack",
    )(profile_index, diffusivity, initial_samples, courant_east, northward_courant)

    obs = observations.reshape(rows, 8, 8, 16).transpose(0, 2, 1, 3).reshape(rows, 8, LANES)
    tile_hot = patch_tiles == jnp.arange(localization.shape[0], dtype=jnp.int32)[None]
    weight = jnp.sum(jnp.where(tile_hot[:, :, None], localization[None], 0.0), axis=1)
    weight = jnp.where(jnp.arange(PATCH * PATCH, dtype=jnp.int32)[None] < patch_counts, weight, 0.0)
    root = jnp.sqrt(weight).reshape(rows, 2, 8, 16).transpose(0, 2, 1, 3).reshape(rows, 8, 32)
    root = jnp.pad(root, ((0, 0), (0, 0), (0, LANES - 32)))
    notes = jnp.stack([obs, root], axis=1)

    both = ("slab", "grp")
    near = [[(r * ROWS + i) * groups + g for g in range(groups) for i in range(ROWS)] for r in range(rows)]
    slab_far = [[r * ROWS + i for r in range(rows)] for i in range(ROWS)]
    rise = [(s, s + ROWS) for s in range(slabs - ROWS)]
    fall = [(s + ROWS, s) for s in range(slabs - ROWS)]

    home_of = [
        (f, ((f % 8) * ROWS + (f // 8) % ROWS) * groups + f // (8 * ROWS)) for f in range(slabs * groups)
    ]
    notes = lax.ppermute(notes, both, home_of)
    spread = pl.pallas_call(
        spread_kernel,
        out_shape=jax.ShapeDtypeStruct((rows, 10, 8, LANES), F32),
        in_specs=[vmem],
        out_specs=vmem,
        compiler_params=params,
        name="spread",
    )(notes)
    sent, spread = lax.optimization_barrier((sent, spread))
    got_m = lax.psum_scatter(spread, "slab", scatter_dimension=0, axis_index_groups=slab_far)

    got = lax.all_to_all(sent, both, 0, 0, axis_index_groups=near, tiled=True)
    got = got.reshape(groups, ROWS, 10, 4, LANES)
    low = lax.ppermute(got[:, ROWS - 1], "slab", rise)
    high = lax.ppermute(got[:, 0], "slab", fall)

    analysed = pl.pallas_call(
        functools.partial(analysis_kernel, groups, slabs),
        out_shape=jax.ShapeDtypeStruct((groups, ROWS, 8, 4, LANES), BF16),
        in_specs=[smem] + [vmem] * 4,
        out_specs=vmem,
        scratch_shapes=[
            pltpu.VMEM((80, members, LANES), F32),
            pltpu.VMEM((10, members, LANES), F32),
            pltpu.VMEM((10, members, LANES), F32),
            pltpu.VMEM((72, members, LANES), F32),
            pltpu.VMEM((8, members, 8 * LANES), BF16),
            pltpu.VMEM((8, PAD, 8 * LANES), BF16),
            pltpu.VMEM((2 * members, 8 * PAD), BF16),
            pltpu.VMEM((10, 24, LANES), F32),
        ],
        compiler_params=params,
        name="analysis",
    )(jnp.sqrt(error_precision), got, low, high, got_m)

    home = lax.all_to_all(
        analysed.reshape(blocks, 8, 4, LANES), both, 0, 0, axis_index_groups=near, tiled=True
    )

    return pl.pallas_call(
        unpack_kernel,
        out_shape=jax.ShapeDtypeStruct((4, 2, 4, blocks * LANES), BF16),
        in_specs=[vmem],
        out_specs=vmem,
        compiler_params=params,
        name="unpack",
    )(home)


def solution(mesh):
    return jax.shard_map(
        on_device,
        mesh=mesh,
        in_specs=(
            P("grp", "slab", None, None),
            P("slab", None, None),
            P("slab", None, None),
            P(),
            P("slab"),
            P(None, None, ("slab", "grp")),
            P(),
            P(),
            P(None, ("slab", "grp")),
            P(None, ("slab", "grp")),
        ),
        out_specs=P("grp", "slab", None, None),
        check_vma=False,
    )
```

```python
import functools
import math

import jax
import jax.numpy as jnp
from jax import lax
from jax.experimental import pallas as pl
from jax.experimental.pallas import tpu as pltpu
from jax.sharding import PartitionSpec as P

PATCH = 16
NS_ITERS = 4
F32 = jnp.float32
BF16 = jnp.bfloat16
VMEM_LIMIT = 56 * 1024 * 1024
LANES = 128
ROWS = 8
PAD = 64


def lane_ids(rows):
    return lax.broadcasted_iota(jnp.int32, (rows, LANES), 1)


def pack_kernel(groups, prof_ref, diff_ref, x_ref, ce_ref, cn_ref, s_ref, turned):
    blocks = ROWS * groups
    me = lax.axis_index("grp")
    part = lax.rem(me // 4, 3)
    kind = lax.rem(me, 4)
    lane4 = lane_ids(4)

    def place(b):
        return pl.ds(pl.multiple_of(b * LANES, LANES), LANES)

    lane8 = lane_ids(8)
    sub8 = lax.rem(lax.broadcasted_iota(jnp.int32, (8, LANES), 0), 4)

    def one(b, carry):
        at = place(b)
        x = [jnp.concatenate([x_ref[m, 0, :, at].astype(F32), x_ref[m, 1, :, at].astype(F32)], axis=0) for m in range(4)]
        for v in range(4):
            tile = x[v]
            for m in range(4):
                if m != v:
                    tile = jnp.where(sub8 == m, pltpu.roll(x[m], (m - v) % 8, 0), tile)
            turned[b, v] = tile
            s_ref[b, v] = tile[0:4].astype(BF16)
            s_ref[b, 4 + v] = tile[4:8].astype(BF16)
        return carry

    lax.fori_loop(0, blocks, one, 0, unroll=4)

    def edges(b, carry):
        before = lax.rem(b + blocks - 1, blocks)
        after = lax.rem(b + 1, blocks)
        packed = jnp.zeros((8, LANES), F32)
        for v in range(4):
            mixed = jnp.where(lane8 < 64, turned[after, v], turned[before, v])
            moved = pltpu.roll(mixed, 2 + 8 * v, 1)
            packed = jnp.where((lane8 >= 8 * v) & (lane8 < 8 * v + 4), moved, packed)
        packed = packed + pltpu.roll(pltpu.roll(packed, 4, 0), 32, 1)
        s_ref[b, 8] = packed[0:4].astype(BF16)
        return carry

    lax.fori_loop(0, blocks, edges, 0, unroll=4)

    def term(x):
        high = x.astype(BF16).astype(F32)
        rest = x - high
        middle = rest.astype(BF16).astype(F32)
        return jnp.where(part == 0, high, jnp.where(part == 1, middle, rest - middle)).astype(BF16)

    def whole(ref, at):
        return jnp.concatenate([ref[0, :, at], ref[1, :, at]], axis=0)

    def plain(ref):
        def go(b, carry):
            s_ref[b, 9] = term(whole(ref, place(b)))
            return carry

        lax.fori_loop(0, blocks, go, 0, unroll=4)

    @pl.when(kind == 0)
    def _():
        plain(ce_ref)

    @pl.when(kind == 1)
    def _():
        plain(cn_ref)

    @pl.when(kind == 2)
    def _():
        lane1 = lane_ids(1)
        kappa_lanes = jnp.zeros((1, LANES), F32)
        for k in range(8):
            value = diff_ref[prof_ref[k // 4], k % 4]
            kappa_lanes = jnp.where(lane1 // 8 == k, value, kappa_lanes)
        sub4 = lax.broadcasted_iota(jnp.int32, (4, LANES), 0)
        mine = (sub4 == lane4 // 16) & (lane4 < 64)
        low_at = lax.rem(lane4, 8) == 1

        def go(b, carry):
            before = place(lax.rem(b + blocks - 1, blocks))
            after = place(lax.rem(b + 1, blocks))
            rows = []
            for ref in (ce_ref, cn_ref):
                low = jnp.broadcast_to(whole(ref, before)[:, LANES - 1 : LANES], (4, LANES))
                high = jnp.broadcast_to(whole(ref, after)[:, 0:1], (4, LANES))
                side = jnp.where(mine, jnp.where(low_at, low, high), 0.0)
                rows.append(jnp.sum(side, axis=0, keepdims=True))
            s_ref[b, 9] = term(jnp.concatenate(rows + [kappa_lanes, jnp.zeros((1, LANES), F32)], axis=0))
            return carry

        lax.fori_loop(0, blocks, go, 0, unroll=4)

    @pl.when(kind == 3)
    def _():
        def go(b, carry):
            s_ref[b, 9] = jnp.zeros((4, LANES), BF16)
            return carry

        lax.fori_loop(0, blocks, go, 0, unroll=4)


def analysis_kernel(
    groups, slabs, ep_ref, r_ref, low_ref, high_ref, rm_ref,
    y_ref, x0, hx, hs, x1, bg, dev, wts, rc_ref
):
    members = 4 * groups
    slab = lax.axis_index("slab")
    row = slab // ROWS
    has_low = row > 0
    has_high = row < slabs // ROWS - 1
    lane = lane_ids(members)
    lane1 = lane_ids(1)


    def coefs(s, ce, cn, kappa):
        east = kappa - 0.5 * ce
        west = kappa + 0.5 * ce
        north = kappa - 0.5 * cn
        south = kappa + 0.5 * cn
        return 1.0 - 4.0 * kappa, east, west, north, south

    def outside(s):
        return ((s == 0) & jnp.logical_not(has_low)) | ((s == 9) & jnp.logical_not(has_high))

    def load(s, read, gone):
        def whole(k):
            x = read(k).astype(F32).reshape(members, LANES)
            return x if gone is None else jnp.where(gone, 0.0, x)

        edge = whole(8)
        for k in range(8):
            x = whole(k)
            x0[s * 8 + k] = x
            own = pltpu.roll(x, 8 * k + 5, 1)
            edge = jnp.where((lane == 8 * k + 4) | (lane == 8 * k + 5), own, edge)
        hs[s] = edge
        rows = whole(9)
        rows = rows[0:16] + rows[16:32] + rows[32:48]
        rc_ref[s, 0:16] = rows
        rc_ref[s, 16:24] = jnp.concatenate(
            [jnp.broadcast_to(rows[10:11, 8 * k : 8 * k + 1], (1, LANES)) for k in range(8)], axis=0
        )

    def load_own(s, carry):
        load(s, lambda k: r_ref[:, s - 1, k], None)
        return carry

    load(0, lambda k: low_ref[:, k], jnp.logical_not(has_low))
    lax.fori_loop(1, 9, load_own, 0, unroll=2)
    load(9, lambda k: high_ref[:, k], jnp.logical_not(has_high))
    half = lane < 64
    packed = [jnp.where(half, hs[2 * q], pltpu.roll(hs[2 * q + 1], 64, 1)) for q in range(5)]

    def pair(a, b):
        return jnp.where(lane1 < 64, a, pltpu.roll(b, 64, 1))

    def swap(x):
        return jnp.where(lax.rem(lane, 8) == 1, pltpu.roll(x, LANES - 1, 1), pltpu.roll(x, 1, 1))

    for q in range(5):
        hx[q] = swap(packed[q])
    stepped = []
    for q in range(5):
        x = packed[q]
        nxt = packed[min(q + 1, 4)]
        prv = packed[max(q - 1, 0)]
        north = jnp.where(lane < 96, pltpu.roll(x, 96, 1), pltpu.roll(nxt, 96, 1))
        south = jnp.where(lane >= 32, pltpu.roll(x, 32, 1), pltpu.roll(prv, 32, 1))
        low = lax.rem(lane, 8) == 1
        east = jnp.where(low, pltpu.roll(x, LANES - 4, 1), pltpu.roll(x, LANES - 1, 1))
        west = jnp.where(low, pltpu.roll(x, 1, 1), pltpu.roll(x, LANES - 2, 1))
        both = [pair(rc_ref[2 * q, 8 + n : 9 + n], rc_ref[2 * q + 1, 8 + n : 9 + n]) for n in range(3)]
        cc, ke, kw, kn, ks = coefs(0, *both)
        new = x * cc + east * ke + west * kw + north * kn + south * ks
        if q == 0:
            new = jnp.where(half & jnp.logical_not(has_low), 0.0, new)
        if q == 4:
            new = jnp.where(jnp.logical_not(half) & jnp.logical_not(has_high), 0.0, new)
        stepped.append(new)
    for q in range(5):
        hx[5 + q] = swap(stepped[q])

    def advance(src, edge_at, t, s, r, v, offset):
        x = src[t - offset * 4]
        north = src[t + 4 - offset * 4]
        south = src[t - 4 - offset * 4]
        base = lax.rem(t, 16) * 8
        edge = pltpu.roll(hx[edge_at + t // 16], lax.rem(254 - base, LANES), 1)
        west = jnp.where(lane == 0, edge, pltpu.roll(x, 1, 1))
        east = jnp.where(lane == LANES - 1, edge, pltpu.roll(x, LANES - 1, 1))
        ce = rc_ref[s, pl.ds(2 * r + v // 2, 1)]
        cn = rc_ref[s, pl.ds(4 + 2 * r + v // 2, 1)]
        kappa = rc_ref[s, pl.ds(16 + 4 * r + v, 1)]
        cc, ke, kw, kn, ks = coefs(0, ce, cn, kappa)
        return x * cc + east * ke + west * kw + north * kn + south * ks

    def first(n, carry):
        s = n // 2
        r = lax.rem(n, 2)
        gone = outside(s)
        for v in range(4):
            new = advance(x0, 0, n * 4 + v, s, r, v, 0)
            x1[n * 4 + v - 4] = jnp.where(gone, 0.0, new)
        return carry

    lax.fori_loop(1, 19, first, 0, unroll=2)

    lane8 = lane_ids(8)
    obs, root_w = [], []
    for a in range(10):
        tile = jnp.zeros((8, LANES), F32)
        for q in range(8):
            tile = jnp.where(lane8 // 16 == q, pltpu.roll(rm_ref[q, a // 8], (16 * (q - a % 8)) % LANES, 1), tile)
        (obs if a < 8 else root_w).append(tile)

    for c in range(8):
        for r in range(2):
            rho = 2 * c + r
            for v in range(4):
                t = (rho + 2) * 4 + v
                new = advance(x1, 5, t, c + 1, r, v, 1)
                rounded = new.astype(BF16)
                back = rounded.astype(F32)
                k = r * 4 + v
                at = slice(k * LANES, (k + 1) * LANES)
                bg[c, :, at] = rounded
                average = jnp.sum(back, axis=0, keepdims=True) * (1.0 / members)
                scale = root_w[rho // 8][rho % 8 : rho % 8 + 1] * ep_ref[v]
                tt = rho * 4 + v
                misfit = (obs[tt // 8][tt % 8 : tt % 8 + 1] - average) * scale
                dev[c, 0:members, at] = ((back - average) * scale).astype(BF16)
                dev[c, members:PAD, at] = jnp.concatenate(
                    [misfit, jnp.zeros((PAD - members - 1, LANES), F32)], axis=0
                ).astype(BF16)

    wide = lax.broadcasted_iota(jnp.int32, (PAD, 8 * LANES), 1)
    strip_of = lax.rem(wide, LANES) // 16

    def gram(c, acc):
        a = dev[c]
        zero = jnp.zeros_like(a)
        stack = jnp.concatenate([jnp.where(strip_of == p, a, zero) for p in range(8)], axis=0)
        return acc + lax.dot_general(stack, a, (((1,), (1,)), ((), ())), preferred_element_type=F32)

    grams = lax.fori_loop(0, 8, gram, jnp.zeros((8 * PAD, PAD), F32))

    si = lax.broadcasted_iota(jnp.int32, (PAD, PAD), 0)
    li = lax.broadcasted_iota(jnp.int32, (PAD, PAD), 1)
    inside = (si < members) & (li < members)
    eye = jnp.where((si == li) & inside, 1.0, 0.0)
    dot = functools.partial(jnp.dot, preferred_element_type=F32, precision=lax.Precision.HIGHEST)
    zs, ys, traces = [], [], []
    for p in range(8):
        full = grams[p * PAD : (p + 1) * PAD]
        system = jnp.where(inside, full, 0.0) + (members - 1.0) * eye
        trace = jnp.sum(jnp.sum(system * eye, axis=1, keepdims=True), axis=0, keepdims=True)
        traces.append(trace)
        ys.append(system / trace)
        zs.append(eye)
    for sweep in range(NS_ITERS):
        cs = []
        for p in range(8):
            zy = ys[p] if sweep == 0 else dot(zs[p], ys[p])
            cs.append(1.5 * eye - 0.5 * zy)
        for p in range(8):
            if sweep < NS_ITERS - 1:
                ys[p] = dot(ys[p], cs[p])
            zs[p] = cs[p] if sweep == 0 else dot(cs[p], zs[p])
    heads, tails = [], []
    for p in range(8):
        full = grams[p * PAD : (p + 1) * PAD]
        root = zs[p] / jnp.sqrt(traces[p])
        drive = jnp.where(li[0:1] < members, full[members : members + 1], 0.0)
        first_col = jnp.sum(root * drive, axis=1, keepdims=True)
        mean_row = jnp.sum(root * first_col, axis=0, keepdims=True)
        w = math.sqrt(members - 1.0) * root + mean_row
        total = jnp.sum(w, axis=1, keepdims=True)
        w = jnp.where(inside, w + (1.0 - total) * (1.0 / members), 0.0)[0:members]
        head = w.astype(BF16)
        heads.append(head.astype(F32))
        tails.append(w - head.astype(F32))
    wts[0:members] = jnp.concatenate(heads, axis=1).astype(BF16)
    wts[members : 2 * members] = jnp.concatenate(tails, axis=1).astype(BF16)

    wide2 = lax.broadcasted_iota(jnp.int32, (members, 2 * LANES), 1)
    strip2 = lax.rem(wide2, LANES) // 16
    fill = jnp.zeros((PAD - members, 2 * LANES), BF16)

    def combine(c, carry):
        for pair_at in range(4):
            b = bg[c, :, pair_at * 2 * LANES : (pair_at + 1) * 2 * LANES]
            zero = jnp.zeros_like(b)
            parts = []
            for p in range(8):
                parts += [jnp.where(strip2 == p, b, zero), fill]
            stack = jnp.concatenate(parts, axis=0)
            out = jnp.dot(wts[...], stack, preferred_element_type=F32)
            out = out[0:members] + out[members : 2 * members]
            for k in range(2):
                y_ref[:, c, pair_at * 2 + k] = (
                    out[:, k * LANES : (k + 1) * LANES].reshape(groups, 4, LANES).astype(BF16)
                )
        return carry

    lax.fori_loop(0, 8, combine, 0)


def unpack_kernel(o_ref, out_ref):
    def one(b, carry):
        at = pl.ds(pl.multiple_of(b * LANES, LANES), LANES)
        for r in range(2):
            x = [o_ref[b, r * 4 + v].astype(F32) for v in range(4)]
            for m in range(4):
                out_ref[m, r, :, at] = jnp.concatenate(
                    [x[v][m : m + 1] for v in range(4)], axis=0
                ).astype(BF16)
        return carry

    lax.fori_loop(0, o_ref.shape[0], one, 0)


def on_device(
    initial_samples,
    courant_east,
    northward_courant,
    diffusivity,
    profile_index,
    observations,
    error_precision,
    localization,
    patch_tiles,
    patch_counts,
):
    slabs = lax.axis_size("slab")
    groups = lax.axis_size("grp")
    blocks = ROWS * groups
    rows = slabs // ROWS
    members = 4 * groups
    vmem = pl.BlockSpec(memory_space=pltpu.VMEM)
    smem = pl.BlockSpec(memory_space=pltpu.SMEM)
    params = pltpu.CompilerParams(vmem_limit_bytes=VMEM_LIMIT)

    sent = pl.pallas_call(
        functools.partial(pack_kernel, groups),
        out_shape=jax.ShapeDtypeStruct((blocks, 10, 4, LANES), BF16),
        in_specs=[smem, smem, vmem, vmem, vmem],
        out_specs=vmem,
        scratch_shapes=[pltpu.VMEM((blocks, 4, 8, LANES), F32)],
        compiler_params=params,
        name="pack",
    )(profile_index, diffusivity, initial_samples, courant_east, northward_courant)

    obs = observations.reshape(rows, 8, 8, 16).transpose(0, 2, 1, 3).reshape(rows, 8, LANES)
    tile_hot = patch_tiles == jnp.arange(localization.shape[0], dtype=jnp.int32)[None]
    weight = jnp.sum(jnp.where(tile_hot[:, :, None], localization[None], 0.0), axis=1)
    weight = jnp.where(jnp.arange(PATCH * PATCH, dtype=jnp.int32)[None] < patch_counts, weight, 0.0)
    root = jnp.sqrt(weight).reshape(rows, 2, 8, 16).transpose(0, 2, 1, 3).reshape(rows, 8, 32)
    root = jnp.pad(root, ((0, 0), (0, 0), (0, LANES - 32)))
    notes = jnp.stack([obs, root], axis=1)

    both = ("slab", "grp")
    near = [[(r * ROWS + i) * groups + g for g in range(groups) for i in range(ROWS)] for r in range(rows)]
    slab_far = [[r * ROWS + i for r in range(rows)] for i in range(ROWS)]
    rise = [(s, s + ROWS) for s in range(slabs - ROWS)]
    fall = [(s + ROWS, s) for s in range(slabs - ROWS)]

    home_of = [
        (f, ((f % 8) * ROWS + (f // 8) % ROWS) * groups + f // (8 * ROWS)) for f in range(slabs * groups)
    ]
    notes = lax.ppermute(notes, both, home_of)
    got_m = lax.all_to_all(notes, "slab", 0, 0, axis_index_groups=slab_far, tiled=True)
    got = lax.all_to_all(sent, both, 0, 0, axis_index_groups=near, tiled=True)
    got = got.reshape(groups, ROWS, 10, 4, LANES)
    low = lax.ppermute(got[:, ROWS - 1], "slab", rise)
    high = lax.ppermute(got[:, 0], "slab", fall)

    analysed = pl.pallas_call(
        functools.partial(analysis_kernel, groups, slabs),
        out_shape=jax.ShapeDtypeStruct((groups, ROWS, 8, 4, LANES), BF16),
        in_specs=[smem] + [vmem] * 4,
        out_specs=vmem,
        scratch_shapes=[
            pltpu.VMEM((80, members, LANES), F32),
            pltpu.VMEM((10, members, LANES), F32),
            pltpu.VMEM((10, members, LANES), F32),
            pltpu.VMEM((72, members, LANES), F32),
            pltpu.VMEM((8, members, 8 * LANES), BF16),
            pltpu.VMEM((8, PAD, 8 * LANES), BF16),
            pltpu.VMEM((2 * members, 8 * PAD), BF16),
            pltpu.VMEM((10, 24, LANES), F32),
        ],
        compiler_params=params,
        name="analysis",
    )(jnp.sqrt(error_precision), got, low, high, got_m)

    home = lax.all_to_all(
        analysed.reshape(blocks, 8, 4, LANES), both, 0, 0, axis_index_groups=near, tiled=True
    )

    return pl.pallas_call(
        unpack_kernel,
        out_shape=jax.ShapeDtypeStruct((4, 2, 4, blocks * LANES), BF16),
        in_specs=[vmem],
        out_specs=vmem,
        compiler_params=params,
        name="unpack",
    )(home)


def solution(mesh):
    return jax.shard_map(
        on_device,
        mesh=mesh,
        in_specs=(
            P("grp", "slab", None, None),
            P("slab", None, None),
            P("slab", None, None),
            P(),
            P("slab"),
            P(None, None, ("slab", "grp")),
            P(),
            P(),
            P(None, ("slab", "grp")),
            P(None, ("slab", "grp")),
        ),
        out_specs=P("grp", "slab", None, None),
        check_vma=False,
    )
```

```python
import functools
import math

import jax
import jax.numpy as jnp
from jax import lax
from jax.experimental import pallas as pl
from jax.experimental.pallas import tpu as pltpu
from jax.sharding import PartitionSpec as P

PATCH = 16
NS_ITERS = 4
F32 = jnp.float32
BF16 = jnp.bfloat16
VMEM_LIMIT = 56 * 1024 * 1024
LANES = 128
ROWS = 8
PAD = 64


def lane_ids(rows):
    return lax.broadcasted_iota(jnp.int32, (rows, LANES), 1)


def pack_kernel(groups, prof_ref, diff_ref, x_ref, ce_ref, cn_ref, s_ref, turned):
    blocks = ROWS * groups
    me = lax.axis_index("grp")
    part = lax.rem(me // 4, 3)
    kind = lax.rem(me, 4)
    lane4 = lane_ids(4)

    def place(b):
        return pl.ds(pl.multiple_of(b * LANES, LANES), LANES)

    lane8 = lane_ids(8)
    sub8 = lax.rem(lax.broadcasted_iota(jnp.int32, (8, LANES), 0), 4)

    def one(b, carry):
        at = place(b)
        x = [jnp.concatenate([x_ref[m, 0, :, at].astype(F32), x_ref[m, 1, :, at].astype(F32)], axis=0) for m in range(4)]
        for v in range(4):
            tile = x[v]
            for m in range(4):
                if m != v:
                    tile = jnp.where(sub8 == m, pltpu.roll(x[m], (m - v) % 8, 0), tile)
            turned[b, v] = tile
            s_ref[b, v] = tile[0:4].astype(BF16)
            s_ref[b, 4 + v] = tile[4:8].astype(BF16)
        return carry

    lax.fori_loop(0, blocks, one, 0, unroll=4)

    def edges(b, carry):
        before = lax.rem(b + blocks - 1, blocks)
        after = lax.rem(b + 1, blocks)
        packed = jnp.zeros((8, LANES), F32)
        for v in range(4):
            mixed = jnp.where(lane8 < 64, turned[after, v], turned[before, v])
            moved = pltpu.roll(mixed, 2 + 8 * v, 1)
            packed = jnp.where((lane8 >= 8 * v) & (lane8 < 8 * v + 4), moved, packed)
        packed = packed + pltpu.roll(pltpu.roll(packed, 4, 0), 32, 1)
        s_ref[b, 8] = packed[0:4].astype(BF16)
        return carry

    lax.fori_loop(0, blocks, edges, 0, unroll=4)

    def term(x):
        high = x.astype(BF16).astype(F32)
        rest = x - high
        middle = rest.astype(BF16).astype(F32)
        return jnp.where(part == 0, high, jnp.where(part == 1, middle, rest - middle)).astype(BF16)

    def whole(ref, at):
        return jnp.concatenate([ref[0, :, at], ref[1, :, at]], axis=0)

    def plain(ref):
        def go(b, carry):
            s_ref[b, 9] = term(whole(ref, place(b)))
            return carry

        lax.fori_loop(0, blocks, go, 0, unroll=4)

    @pl.when(kind == 0)
    def _():
        plain(ce_ref)

    @pl.when(kind == 1)
    def _():
        plain(cn_ref)

    @pl.when(kind == 2)
    def _():
        lane1 = lane_ids(1)
        kappa_lanes = jnp.zeros((1, LANES), F32)
        for k in range(8):
            value = diff_ref[prof_ref[k // 4], k % 4]
            kappa_lanes = jnp.where(lane1 // 8 == k, value, kappa_lanes)
        sub4 = lax.broadcasted_iota(jnp.int32, (4, LANES), 0)
        mine = (sub4 == lane4 // 16) & (lane4 < 64)
        low_at = lax.rem(lane4, 8) == 1

        def go(b, carry):
            before = place(lax.rem(b + blocks - 1, blocks))
            after = place(lax.rem(b + 1, blocks))
            rows = []
            for ref in (ce_ref, cn_ref):
                low = jnp.broadcast_to(whole(ref, before)[:, LANES - 1 : LANES], (4, LANES))
                high = jnp.broadcast_to(whole(ref, after)[:, 0:1], (4, LANES))
                side = jnp.where(mine, jnp.where(low_at, low, high), 0.0)
                rows.append(jnp.sum(side, axis=0, keepdims=True))
            s_ref[b, 9] = term(jnp.concatenate(rows + [kappa_lanes, jnp.zeros((1, LANES), F32)], axis=0))
            return carry

        lax.fori_loop(0, blocks, go, 0, unroll=4)

    @pl.when(kind == 3)
    def _():
        def go(b, carry):
            s_ref[b, 9] = jnp.zeros((4, LANES), BF16)
            return carry

        lax.fori_loop(0, blocks, go, 0, unroll=4)


def analysis_kernel(
    groups, slabs, ep_ref, r_ref, low_ref, high_ref, *refs):
    rounds = refs[:8]
    y_ref, x0, hx, hs, x1, bg, dev, wts, rc_ref, rm_ref = refs[8:]
    for k in range(8):
        rm_ref[lax.rem(lax.axis_index("slab") // ROWS + 8 - k, 8)] = rounds[k][...]
    members = 4 * groups
    slab = lax.axis_index("slab")
    row = slab // ROWS
    has_low = row > 0
    has_high = row < slabs // ROWS - 1
    lane = lane_ids(members)
    lane1 = lane_ids(1)


    def coefs(s, ce, cn, kappa):
        east = kappa - 0.5 * ce
        west = kappa + 0.5 * ce
        north = kappa - 0.5 * cn
        south = kappa + 0.5 * cn
        return 1.0 - 4.0 * kappa, east, west, north, south

    def outside(s):
        return ((s == 0) & jnp.logical_not(has_low)) | ((s == 9) & jnp.logical_not(has_high))

    def load(s, read, gone):
        def whole(k):
            x = read(k).astype(F32).reshape(members, LANES)
            return x if gone is None else jnp.where(gone, 0.0, x)

        edge = whole(8)
        for k in range(8):
            x = whole(k)
            x0[s * 8 + k] = x
            own = pltpu.roll(x, 8 * k + 5, 1)
            edge = jnp.where((lane == 8 * k + 4) | (lane == 8 * k + 5), own, edge)
        hs[s] = edge
        rows = whole(9)
        rows = rows[0:16] + rows[16:32] + rows[32:48]
        rc_ref[s, 0:16] = rows
        rc_ref[s, 16:24] = jnp.concatenate(
            [jnp.broadcast_to(rows[10:11, 8 * k : 8 * k + 1], (1, LANES)) for k in range(8)], axis=0
        )

    def load_own(s, carry):
        load(s, lambda k: r_ref[:, s - 1, k], None)
        return carry

    load(0, lambda k: low_ref[:, k], jnp.logical_not(has_low))
    lax.fori_loop(1, 9, load_own, 0, unroll=2)
    load(9, lambda k: high_ref[:, k], jnp.logical_not(has_high))
    half = lane < 64
    packed = [jnp.where(half, hs[2 * q], pltpu.roll(hs[2 * q + 1], 64, 1)) for q in range(5)]

    def pair(a, b):
        return jnp.where(lane1 < 64, a, pltpu.roll(b, 64, 1))

    def swap(x):
        return jnp.where(lax.rem(lane, 8) == 1, pltpu.roll(x, LANES - 1, 1), pltpu.roll(x, 1, 1))

    for q in range(5):
        hx[q] = swap(packed[q])
    stepped = []
    for q in range(5):
        x = packed[q]
        nxt = packed[min(q + 1, 4)]
        prv = packed[max(q - 1, 0)]
        north = jnp.where(lane < 96, pltpu.roll(x, 96, 1), pltpu.roll(nxt, 96, 1))
        south = jnp.where(lane >= 32, pltpu.roll(x, 32, 1), pltpu.roll(prv, 32, 1))
        low = lax.rem(lane, 8) == 1
        east = jnp.where(low, pltpu.roll(x, LANES - 4, 1), pltpu.roll(x, LANES - 1, 1))
        west = jnp.where(low, pltpu.roll(x, 1, 1), pltpu.roll(x, LANES - 2, 1))
        both = [pair(rc_ref[2 * q, 8 + n : 9 + n], rc_ref[2 * q + 1, 8 + n : 9 + n]) for n in range(3)]
        cc, ke, kw, kn, ks = coefs(0, *both)
        new = x * cc + east * ke + west * kw + north * kn + south * ks
        if q == 0:
            new = jnp.where(half & jnp.logical_not(has_low), 0.0, new)
        if q == 4:
            new = jnp.where(jnp.logical_not(half) & jnp.logical_not(has_high), 0.0, new)
        stepped.append(new)
    for q in range(5):
        hx[5 + q] = swap(stepped[q])

    def advance(src, edge_at, t, s, r, v, offset):
        x = src[t - offset * 4]
        north = src[t + 4 - offset * 4]
        south = src[t - 4 - offset * 4]
        base = lax.rem(t, 16) * 8
        edge = pltpu.roll(hx[edge_at + t // 16], lax.rem(254 - base, LANES), 1)
        west = jnp.where(lane == 0, edge, pltpu.roll(x, 1, 1))
        east = jnp.where(lane == LANES - 1, edge, pltpu.roll(x, LANES - 1, 1))
        ce = rc_ref[s, pl.ds(2 * r + v // 2, 1)]
        cn = rc_ref[s, pl.ds(4 + 2 * r + v // 2, 1)]
        kappa = rc_ref[s, pl.ds(16 + 4 * r + v, 1)]
        cc, ke, kw, kn, ks = coefs(0, ce, cn, kappa)
        return x * cc + east * ke + west * kw + north * kn + south * ks

    def first(n, carry):
        s = n // 2
        r = lax.rem(n, 2)
        gone = outside(s)
        for v in range(4):
            new = advance(x0, 0, n * 4 + v, s, r, v, 0)
            x1[n * 4 + v - 4] = jnp.where(gone, 0.0, new)
        return carry

    lax.fori_loop(1, 19, first, 0, unroll=2)

    lane8 = lane_ids(8)
    obs, root_w = [], []
    for a in range(10):
        tile = jnp.zeros((8, LANES), F32)
        for q in range(8):
            tile = jnp.where(lane8 // 16 == q, pltpu.roll(rm_ref[q, a // 8], (16 * (q - a % 8)) % LANES, 1), tile)
        (obs if a < 8 else root_w).append(tile)

    for c in range(8):
        for r in range(2):
            rho = 2 * c + r
            for v in range(4):
                t = (rho + 2) * 4 + v
                new = advance(x1, 5, t, c + 1, r, v, 1)
                rounded = new.astype(BF16)
                back = rounded.astype(F32)
                k = r * 4 + v
                at = slice(k * LANES, (k + 1) * LANES)
                bg[c, :, at] = rounded
                average = jnp.sum(back, axis=0, keepdims=True) * (1.0 / members)
                scale = root_w[rho // 8][rho % 8 : rho % 8 + 1] * ep_ref[v]
                tt = rho * 4 + v
                misfit = (obs[tt // 8][tt % 8 : tt % 8 + 1] - average) * scale
                dev[c, 0:members, at] = ((back - average) * scale).astype(BF16)
                dev[c, members:PAD, at] = jnp.concatenate(
                    [misfit, jnp.zeros((PAD - members - 1, LANES), F32)], axis=0
                ).astype(BF16)

    wide = lax.broadcasted_iota(jnp.int32, (PAD, 8 * LANES), 1)
    strip_of = lax.rem(wide, LANES) // 16

    def gram(c, acc):
        a = dev[c]
        zero = jnp.zeros_like(a)
        stack = jnp.concatenate([jnp.where(strip_of == p, a, zero) for p in range(8)], axis=0)
        return acc + lax.dot_general(stack, a, (((1,), (1,)), ((), ())), preferred_element_type=F32)

    grams = lax.fori_loop(0, 8, gram, jnp.zeros((8 * PAD, PAD), F32))

    si = lax.broadcasted_iota(jnp.int32, (PAD, PAD), 0)
    li = lax.broadcasted_iota(jnp.int32, (PAD, PAD), 1)
    inside = (si < members) & (li < members)
    eye = jnp.where((si == li) & inside, 1.0, 0.0)
    dot = functools.partial(jnp.dot, preferred_element_type=F32, precision=lax.Precision.HIGHEST)
    zs, ys, traces = [], [], []
    for p in range(8):
        full = grams[p * PAD : (p + 1) * PAD]
        system = jnp.where(inside, full, 0.0) + (members - 1.0) * eye
        trace = jnp.sum(jnp.sum(system * eye, axis=1, keepdims=True), axis=0, keepdims=True)
        traces.append(trace)
        ys.append(system / trace)
        zs.append(eye)
    for sweep in range(NS_ITERS):
        cs = []
        for p in range(8):
            zy = ys[p] if sweep == 0 else dot(zs[p], ys[p])
            cs.append(1.5 * eye - 0.5 * zy)
        for p in range(8):
            if sweep < NS_ITERS - 1:
                ys[p] = dot(ys[p], cs[p])
            zs[p] = cs[p] if sweep == 0 else dot(cs[p], zs[p])
    heads, tails = [], []
    for p in range(8):
        full = grams[p * PAD : (p + 1) * PAD]
        root = zs[p] / jnp.sqrt(traces[p])
        drive = jnp.where(li[0:1] < members, full[members : members + 1], 0.0)
        first_col = jnp.sum(root * drive, axis=1, keepdims=True)
        mean_row = jnp.sum(root * first_col, axis=0, keepdims=True)
        w = math.sqrt(members - 1.0) * root + mean_row
        total = jnp.sum(w, axis=1, keepdims=True)
        w = jnp.where(inside, w + (1.0 - total) * (1.0 / members), 0.0)[0:members]
        head = w.astype(BF16)
        heads.append(head.astype(F32))
        tails.append(w - head.astype(F32))
    wts[0:members] = jnp.concatenate(heads, axis=1).astype(BF16)
    wts[members : 2 * members] = jnp.concatenate(tails, axis=1).astype(BF16)

    wide2 = lax.broadcasted_iota(jnp.int32, (members, 2 * LANES), 1)
    strip2 = lax.rem(wide2, LANES) // 16
    fill = jnp.zeros((PAD - members, 2 * LANES), BF16)

    def combine(c, carry):
        for pair_at in range(4):
            b = bg[c, :, pair_at * 2 * LANES : (pair_at + 1) * 2 * LANES]
            zero = jnp.zeros_like(b)
            parts = []
            for p in range(8):
                parts += [jnp.where(strip2 == p, b, zero), fill]
            stack = jnp.concatenate(parts, axis=0)
            out = jnp.dot(wts[...], stack, preferred_element_type=F32)
            out = out[0:members] + out[members : 2 * members]
            for k in range(2):
                y_ref[:, c, pair_at * 2 + k] = (
                    out[:, k * LANES : (k + 1) * LANES].reshape(groups, 4, LANES).astype(BF16)
                )
        return carry

    lax.fori_loop(0, 8, combine, 0)


def unpack_kernel(o_ref, out_ref):
    sub8 = lax.rem(lax.broadcasted_iota(jnp.int32, (8, LANES), 0), 4)

    def one(b, carry):
        at = pl.ds(pl.multiple_of(b * LANES, LANES), LANES)
        x = [jnp.concatenate([o_ref[b, v].astype(F32), o_ref[b, 4 + v].astype(F32)], axis=0) for v in range(4)]
        for m in range(4):
            tile = x[m]
            for v in range(4):
                if m != v:
                    tile = jnp.where(sub8 == v, pltpu.roll(x[v], (v - m) % 8, 0), tile)
            out_ref[m, 0, :, at] = tile[0:4].astype(BF16)
            out_ref[m, 1, :, at] = tile[4:8].astype(BF16)
        return carry

    lax.fori_loop(0, o_ref.shape[0], one, 0, unroll=4)


def on_device(
    initial_samples,
    courant_east,
    northward_courant,
    diffusivity,
    profile_index,
    observations,
    error_precision,
    localization,
    patch_tiles,
    patch_counts,
):
    slabs = lax.axis_size("slab")
    groups = lax.axis_size("grp")
    blocks = ROWS * groups
    rows = slabs // ROWS
    members = 4 * groups
    vmem = pl.BlockSpec(memory_space=pltpu.VMEM)
    smem = pl.BlockSpec(memory_space=pltpu.SMEM)
    params = pltpu.CompilerParams(vmem_limit_bytes=VMEM_LIMIT)

    sent = pl.pallas_call(
        functools.partial(pack_kernel, groups),
        out_shape=jax.ShapeDtypeStruct((blocks, 10, 4, LANES), BF16),
        in_specs=[smem, smem, vmem, vmem, vmem],
        out_specs=vmem,
        scratch_shapes=[pltpu.VMEM((blocks, 4, 8, LANES), F32)],
        compiler_params=params,
        name="pack",
    )(profile_index, diffusivity, initial_samples, courant_east, northward_courant)

    obs = observations.reshape(rows, 8, 8, 16).transpose(0, 2, 1, 3).reshape(rows, 8, LANES)
    tile_hot = patch_tiles == jnp.arange(localization.shape[0], dtype=jnp.int32)[None]
    weight = jnp.sum(jnp.where(tile_hot[:, :, None], localization[None], 0.0), axis=1)
    weight = jnp.where(jnp.arange(PATCH * PATCH, dtype=jnp.int32)[None] < patch_counts, weight, 0.0)
    root = jnp.sqrt(weight).reshape(rows, 2, 8, 16).transpose(0, 2, 1, 3).reshape(rows, 8, 32)
    root = jnp.pad(root, ((0, 0), (0, 0), (0, LANES - 32)))
    notes = jnp.stack([obs, root], axis=1)

    both = ("slab", "grp")
    near = [[(r * ROWS + i) * groups + g for g in range(groups) for i in range(ROWS)] for r in range(rows)]
    rise = [(s, s + ROWS) for s in range(slabs - ROWS)]
    fall = [(s + ROWS, s) for s in range(slabs - ROWS)]

    flat = lax.axis_index("slab") * groups + lax.axis_index("grp")
    turned = lax.dynamic_slice_in_dim(jnp.concatenate([notes, notes]), lax.rem(flat, 8), 8)
    rounds = []
    for k in range(8):
        route = [
            (f, (((f + k) % 8) * ROWS + (f // 8) % ROWS) * groups + f // (8 * ROWS))
            for f in range(slabs * groups)
        ]
        rounds.append(lax.ppermute(turned[k], both, route))
    got = lax.all_to_all(sent, both, 0, 0, axis_index_groups=near, tiled=True)
    got, *rounds = lax.optimization_barrier((got, *rounds))
    got = got.reshape(groups, ROWS, 10, 4, LANES)
    low = lax.ppermute(got[:, ROWS - 1], "slab", rise)
    high = lax.ppermute(got[:, 0], "slab", fall)

    analysed = pl.pallas_call(
        functools.partial(analysis_kernel, groups, slabs),
        out_shape=jax.ShapeDtypeStruct((groups, ROWS, 8, 4, LANES), BF16),
        in_specs=[smem] + [vmem] * 11,
        out_specs=vmem,
        scratch_shapes=[
            pltpu.VMEM((80, members, LANES), F32),
            pltpu.VMEM((10, members, LANES), F32),
            pltpu.VMEM((10, members, LANES), F32),
            pltpu.VMEM((72, members, LANES), F32),
            pltpu.VMEM((8, members, 8 * LANES), BF16),
            pltpu.VMEM((8, PAD, 8 * LANES), BF16),
            pltpu.VMEM((2 * members, 8 * PAD), BF16),
            pltpu.VMEM((10, 24, LANES), F32),
            pltpu.VMEM((8, 2, 8, LANES), F32),
        ],
        compiler_params=params,
        name="analysis",
    )(jnp.sqrt(error_precision), got, low, high, *rounds)

    home = lax.all_to_all(
        analysed.reshape(blocks, 8, 4, LANES), both, 0, 0, axis_index_groups=near, tiled=True
    )

    return pl.pallas_call(
        unpack_kernel,
        out_shape=jax.ShapeDtypeStruct((4, 2, 4, blocks * LANES), BF16),
        in_specs=[vmem],
        out_specs=vmem,
        compiler_params=params,
        name="unpack",
    )(home)


def solution(mesh):
    return jax.shard_map(
        on_device,
        mesh=mesh,
        in_specs=(
            P("grp", "slab", None, None),
            P("slab", None, None),
            P("slab", None, None),
            P(),
            P("slab"),
            P(None, None, ("slab", "grp")),
            P(),
            P(),
            P(None, ("slab", "grp")),
            P(None, ("slab", "grp")),
        ),
        out_specs=P("grp", "slab", None, None),
        check_vma=False,
    )
```

```python
import functools
import math

import jax
import jax.numpy as jnp
from jax import lax
from jax.experimental import pallas as pl
from jax.experimental.pallas import tpu as pltpu
from jax.sharding import PartitionSpec as P

PATCH = 16
NS_ITERS = 4
F32 = jnp.float32
BF16 = jnp.bfloat16
VMEM_LIMIT = 56 * 1024 * 1024
LANES = 128
ROWS = 8
PAD = 64


def lane_ids(rows):
    return lax.broadcasted_iota(jnp.int32, (rows, LANES), 1)


def pack_kernel(groups, prof_ref, diff_ref, x_ref, ce_ref, cn_ref, s_ref, turned):
    blocks = ROWS * groups
    me = lax.axis_index("grp")
    part = lax.rem(me // 4, 3)
    kind = lax.rem(me, 4)
    lane4 = lane_ids(4)

    def place(b):
        return pl.ds(pl.multiple_of(b * LANES, LANES), LANES)

    lane8 = lane_ids(8)
    sub8 = lax.rem(lax.broadcasted_iota(jnp.int32, (8, LANES), 0), 4)

    def one(b, carry):
        at = place(b)
        x = [jnp.concatenate([x_ref[m, 0, :, at].astype(F32), x_ref[m, 1, :, at].astype(F32)], axis=0) for m in range(4)]
        for v in range(4):
            tile = x[v]
            for m in range(4):
                if m != v:
                    tile = jnp.where(sub8 == m, pltpu.roll(x[m], (m - v) % 8, 0), tile)
            turned[b, v] = tile
            s_ref[b, v] = tile[0:4].astype(BF16)
            s_ref[b, 4 + v] = tile[4:8].astype(BF16)
        return carry

    lax.fori_loop(0, blocks, one, 0, unroll=4)

    def edges(b, carry):
        before = lax.rem(b + blocks - 1, blocks)
        after = lax.rem(b + 1, blocks)
        packed = jnp.zeros((8, LANES), F32)
        for v in range(4):
            mixed = jnp.where(lane8 < 64, turned[after, v], turned[before, v])
            moved = pltpu.roll(mixed, 2 + 8 * v, 1)
            packed = jnp.where((lane8 >= 8 * v) & (lane8 < 8 * v + 4), moved, packed)
        packed = packed + pltpu.roll(pltpu.roll(packed, 4, 0), 32, 1)
        s_ref[b, 8] = packed[0:4].astype(BF16)
        return carry

    lax.fori_loop(0, blocks, edges, 0, unroll=4)

    def term(x):
        high = x.astype(BF16).astype(F32)
        rest = x - high
        middle = rest.astype(BF16).astype(F32)
        return jnp.where(part == 0, high, jnp.where(part == 1, middle, rest - middle)).astype(BF16)

    def whole(ref, at):
        return jnp.concatenate([ref[0, :, at], ref[1, :, at]], axis=0)

    def plain(ref):
        def go(b, carry):
            s_ref[b, 9] = term(whole(ref, place(b)))
            return carry

        lax.fori_loop(0, blocks, go, 0, unroll=4)

    @pl.when(kind == 0)
    def _():
        plain(ce_ref)

    @pl.when(kind == 1)
    def _():
        plain(cn_ref)

    @pl.when(kind == 2)
    def _():
        lane1 = lane_ids(1)
        kappa_lanes = jnp.zeros((1, LANES), F32)
        for k in range(8):
            value = diff_ref[prof_ref[k // 4], k % 4]
            kappa_lanes = jnp.where(lane1 // 8 == k, value, kappa_lanes)
        sub4 = lax.broadcasted_iota(jnp.int32, (4, LANES), 0)
        mine = (sub4 == lane4 // 16) & (lane4 < 64)
        low_at = lax.rem(lane4, 8) == 1

        def go(b, carry):
            before = place(lax.rem(b + blocks - 1, blocks))
            after = place(lax.rem(b + 1, blocks))
            rows = []
            for ref in (ce_ref, cn_ref):
                low = jnp.broadcast_to(whole(ref, before)[:, LANES - 1 : LANES], (4, LANES))
                high = jnp.broadcast_to(whole(ref, after)[:, 0:1], (4, LANES))
                side = jnp.where(mine, jnp.where(low_at, low, high), 0.0)
                rows.append(jnp.sum(side, axis=0, keepdims=True))
            s_ref[b, 9] = term(jnp.concatenate(rows + [kappa_lanes, jnp.zeros((1, LANES), F32)], axis=0))
            return carry

        lax.fori_loop(0, blocks, go, 0, unroll=4)

    @pl.when(kind == 3)
    def _():
        def go(b, carry):
            s_ref[b, 9] = jnp.zeros((4, LANES), BF16)
            return carry

        lax.fori_loop(0, blocks, go, 0, unroll=4)


def analysis_kernel(
    groups, slabs, ep_ref, r_ref, low_ref, high_ref, rm_ref,
    y_ref, x0, hx, hs, x1, bg, dev, wts, rc_ref
):
    members = 4 * groups
    slab = lax.axis_index("slab")
    row = slab // ROWS
    has_low = row > 0
    has_high = row < slabs // ROWS - 1
    lane = lane_ids(members)
    lane1 = lane_ids(1)


    def coefs(s, ce, cn, kappa):
        east = kappa - 0.5 * ce
        west = kappa + 0.5 * ce
        north = kappa - 0.5 * cn
        south = kappa + 0.5 * cn
        return 1.0 - 4.0 * kappa, east, west, north, south

    def outside(s):
        return ((s == 0) & jnp.logical_not(has_low)) | ((s == 9) & jnp.logical_not(has_high))

    def load(s, read, gone):
        def whole(k):
            x = read(k).astype(F32).reshape(members, LANES)
            return x if gone is None else jnp.where(gone, 0.0, x)

        edge = whole(8)
        for k in range(8):
            x = whole(k)
            x0[s * 8 + k] = x
            own = pltpu.roll(x, 8 * k + 5, 1)
            edge = jnp.where((lane == 8 * k + 4) | (lane == 8 * k + 5), own, edge)
        hs[s] = edge
        rows = whole(9)
        rows = rows[0:16] + rows[16:32] + rows[32:48]
        rc_ref[s, 0:16] = rows
        rc_ref[s, 16:24] = jnp.concatenate(
            [jnp.broadcast_to(rows[10:11, 8 * k : 8 * k + 1], (1, LANES)) for k in range(8)], axis=0
        )

    def load_own(s, carry):
        load(s, lambda k: r_ref[:, s - 1, k], None)
        return carry

    load(0, lambda k: low_ref[:, k], jnp.logical_not(has_low))
    lax.fori_loop(1, 9, load_own, 0, unroll=2)
    load(9, lambda k: high_ref[:, k], jnp.logical_not(has_high))
    half = lane < 64
    packed = [jnp.where(half, hs[2 * q], pltpu.roll(hs[2 * q + 1], 64, 1)) for q in range(5)]

    def pair(a, b):
        return jnp.where(lane1 < 64, a, pltpu.roll(b, 64, 1))

    def swap(x):
        return jnp.where(lax.rem(lane, 8) == 1, pltpu.roll(x, LANES - 1, 1), pltpu.roll(x, 1, 1))

    for q in range(5):
        hx[q] = swap(packed[q])
    stepped = []
    for q in range(5):
        x = packed[q]
        nxt = packed[min(q + 1, 4)]
        prv = packed[max(q - 1, 0)]
        north = jnp.where(lane < 96, pltpu.roll(x, 96, 1), pltpu.roll(nxt, 96, 1))
        south = jnp.where(lane >= 32, pltpu.roll(x, 32, 1), pltpu.roll(prv, 32, 1))
        low = lax.rem(lane, 8) == 1
        east = jnp.where(low, pltpu.roll(x, LANES - 4, 1), pltpu.roll(x, LANES - 1, 1))
        west = jnp.where(low, pltpu.roll(x, 1, 1), pltpu.roll(x, LANES - 2, 1))
        both = [pair(rc_ref[2 * q, 8 + n : 9 + n], rc_ref[2 * q + 1, 8 + n : 9 + n]) for n in range(3)]
        cc, ke, kw, kn, ks = coefs(0, *both)
        new = x * cc + east * ke + west * kw + north * kn + south * ks
        if q == 0:
            new = jnp.where(half & jnp.logical_not(has_low), 0.0, new)
        if q == 4:
            new = jnp.where(jnp.logical_not(half) & jnp.logical_not(has_high), 0.0, new)
        stepped.append(new)
    for q in range(5):
        hx[5 + q] = swap(stepped[q])

    def advance(src, edge_at, t, s, r, v, offset):
        x = src[t - offset * 4]
        north = src[t + 4 - offset * 4]
        south = src[t - 4 - offset * 4]
        base = lax.rem(t, 16) * 8
        edge = pltpu.roll(hx[edge_at + t // 16], lax.rem(254 - base, LANES), 1)
        west = jnp.where(lane == 0, edge, pltpu.roll(x, 1, 1))
        east = jnp.where(lane == LANES - 1, edge, pltpu.roll(x, LANES - 1, 1))
        ce = rc_ref[s, pl.ds(2 * r + v // 2, 1)]
        cn = rc_ref[s, pl.ds(4 + 2 * r + v // 2, 1)]
        kappa = rc_ref[s, pl.ds(16 + 4 * r + v, 1)]
        cc, ke, kw, kn, ks = coefs(0, ce, cn, kappa)
        return x * cc + east * ke + west * kw + north * kn + south * ks

    def first(n, carry):
        s = n // 2
        r = lax.rem(n, 2)
        gone = outside(s)
        for v in range(4):
            new = advance(x0, 0, n * 4 + v, s, r, v, 0)
            x1[n * 4 + v - 4] = jnp.where(gone, 0.0, new)
        return carry

    lax.fori_loop(1, 19, first, 0, unroll=2)

    lane8 = lane_ids(8)
    obs, root_w = [], []
    for a in range(10):
        tile = jnp.zeros((8, LANES), F32)
        for q in range(8):
            tile = jnp.where(lane8 // 16 == q, pltpu.roll(rm_ref[q, a // 8], (16 * (q - a % 8)) % LANES, 1), tile)
        (obs if a < 8 else root_w).append(tile)

    for c in range(8):
        for r in range(2):
            rho = 2 * c + r
            for v in range(4):
                t = (rho + 2) * 4 + v
                new = advance(x1, 5, t, c + 1, r, v, 1)
                rounded = new.astype(BF16)
                back = rounded.astype(F32)
                k = r * 4 + v
                at = slice(k * LANES, (k + 1) * LANES)
                bg[c, :, at] = rounded
                average = jnp.sum(back, axis=0, keepdims=True) * (1.0 / members)
                scale = root_w[rho // 8][rho % 8 : rho % 8 + 1] * ep_ref[v]
                tt = rho * 4 + v
                misfit = (obs[tt // 8][tt % 8 : tt % 8 + 1] - average) * scale
                dev[c, 0:members, at] = ((back - average) * scale).astype(BF16)
                dev[c, members:PAD, at] = jnp.concatenate(
                    [misfit, jnp.zeros((PAD - members - 1, LANES), F32)], axis=0
                ).astype(BF16)

    wide = lax.broadcasted_iota(jnp.int32, (PAD, 8 * LANES), 1)
    strip_of = lax.rem(wide, LANES) // 16

    def gram(c, acc):
        a = dev[c]
        zero = jnp.zeros_like(a)
        stack = jnp.concatenate([jnp.where(strip_of == p, a, zero) for p in range(8)], axis=0)
        return acc + lax.dot_general(stack, a, (((1,), (1,)), ((), ())), preferred_element_type=F32)

    grams = lax.fori_loop(0, 8, gram, jnp.zeros((8 * PAD, PAD), F32))

    si = lax.broadcasted_iota(jnp.int32, (PAD, PAD), 0)
    li = lax.broadcasted_iota(jnp.int32, (PAD, PAD), 1)
    inside = (si < members) & (li < members)
    eye = jnp.where((si == li) & inside, 1.0, 0.0)
    dot = functools.partial(jnp.dot, preferred_element_type=F32, precision=lax.Precision.HIGHEST)
    zs, ys, traces = [], [], []
    for p in range(8):
        full = grams[p * PAD : (p + 1) * PAD]
        system = jnp.where(inside, full, 0.0) + (members - 1.0) * eye
        trace = jnp.sum(jnp.sum(system * eye, axis=1, keepdims=True), axis=0, keepdims=True)
        traces.append(trace)
        ys.append(system / trace)
        zs.append(eye)
    for sweep in range(NS_ITERS):
        cs = []
        for p in range(8):
            zy = ys[p] if sweep == 0 else dot(zs[p], ys[p])
            cs.append(1.5 * eye - 0.5 * zy)
        for p in range(8):
            if sweep < NS_ITERS - 1:
                ys[p] = dot(ys[p], cs[p])
            zs[p] = cs[p] if sweep == 0 else dot(cs[p], zs[p])
    heads, tails = [], []
    for p in range(8):
        full = grams[p * PAD : (p + 1) * PAD]
        root = zs[p] / jnp.sqrt(traces[p])
        drive = jnp.where(li[0:1] < members, full[members : members + 1], 0.0)
        first_col = jnp.sum(root * drive, axis=1, keepdims=True)
        mean_row = jnp.sum(root * first_col, axis=0, keepdims=True)
        w = math.sqrt(members - 1.0) * root + mean_row
        total = jnp.sum(w, axis=1, keepdims=True)
        w = jnp.where(inside, w + (1.0 - total) * (1.0 / members), 0.0)[0:members]
        head = w.astype(BF16)
        heads.append(head.astype(F32))
        tails.append(w - head.astype(F32))
    wts[0:members] = jnp.concatenate(heads, axis=1).astype(BF16)
    wts[members : 2 * members] = jnp.concatenate(tails, axis=1).astype(BF16)

    wide2 = lax.broadcasted_iota(jnp.int32, (members, 2 * LANES), 1)
    strip2 = lax.rem(wide2, LANES) // 16
    fill = jnp.zeros((PAD - members, 2 * LANES), BF16)

    def combine(c, carry):
        for pair_at in range(4):
            b = bg[c, :, pair_at * 2 * LANES : (pair_at + 1) * 2 * LANES]
            zero = jnp.zeros_like(b)
            parts = []
            for p in range(8):
                parts += [jnp.where(strip2 == p, b, zero), fill]
            stack = jnp.concatenate(parts, axis=0)
            out = jnp.dot(wts[...], stack, preferred_element_type=F32)
            out = out[0:members] + out[members : 2 * members]
            for k in range(2):
                y_ref[:, c, pair_at * 2 + k] = (
                    out[:, k * LANES : (k + 1) * LANES].reshape(groups, 4, LANES).astype(BF16)
                )
        return carry

    lax.fori_loop(0, 8, combine, 0)


def unpack_kernel(o_ref, out_ref):
    sub8 = lax.rem(lax.broadcasted_iota(jnp.int32, (8, LANES), 0), 4)

    def one(b, carry):
        at = pl.ds(pl.multiple_of(b * LANES, LANES), LANES)
        x = [jnp.concatenate([o_ref[b, v].astype(F32), o_ref[b, 4 + v].astype(F32)], axis=0) for v in range(4)]
        for m in range(4):
            tile = x[m]
            for v in range(4):
                if m != v:
                    tile = jnp.where(sub8 == v, pltpu.roll(x[v], (v - m) % 8, 0), tile)
            out_ref[m, 0, :, at] = tile[0:4].astype(BF16)
            out_ref[m, 1, :, at] = tile[4:8].astype(BF16)
        return carry

    lax.fori_loop(0, o_ref.shape[0], one, 0, unroll=4)


def on_device(
    initial_samples,
    courant_east,
    northward_courant,
    diffusivity,
    profile_index,
    observations,
    error_precision,
    localization,
    patch_tiles,
    patch_counts,
):
    slabs = lax.axis_size("slab")
    groups = lax.axis_size("grp")
    blocks = ROWS * groups
    rows = slabs // ROWS
    members = 4 * groups
    vmem = pl.BlockSpec(memory_space=pltpu.VMEM)
    smem = pl.BlockSpec(memory_space=pltpu.SMEM)
    params = pltpu.CompilerParams(vmem_limit_bytes=VMEM_LIMIT)

    sent = pl.pallas_call(
        functools.partial(pack_kernel, groups),
        out_shape=jax.ShapeDtypeStruct((blocks, 10, 4, LANES), BF16),
        in_specs=[smem, smem, vmem, vmem, vmem],
        out_specs=vmem,
        scratch_shapes=[pltpu.VMEM((blocks, 4, 8, LANES), F32)],
        compiler_params=params,
        name="pack",
    )(profile_index, diffusivity, initial_samples, courant_east, northward_courant)

    obs = observations.reshape(rows, 8, 8, 16).transpose(0, 2, 1, 3).reshape(rows, 8, LANES)
    tile_hot = patch_tiles == jnp.arange(localization.shape[0], dtype=jnp.int32)[None]
    weight = jnp.sum(jnp.where(tile_hot[:, :, None], localization[None], 0.0), axis=1)
    weight = jnp.where(jnp.arange(PATCH * PATCH, dtype=jnp.int32)[None] < patch_counts, weight, 0.0)
    root = jnp.sqrt(weight).reshape(rows, 2, 8, 16).transpose(0, 2, 1, 3).reshape(rows, 8, 32)
    root = jnp.pad(root, ((0, 0), (0, 0), (0, LANES - 32)))
    notes = jnp.stack([obs, root], axis=1)

    both = ("slab", "grp")
    near = [[(r * ROWS + i) * groups + g for g in range(groups) for i in range(ROWS)] for r in range(rows)]
    slab_far = [[r * ROWS + i for r in range(rows)] for i in range(ROWS)]
    rise = [(s, s + ROWS) for s in range(slabs - ROWS)]
    fall = [(s + ROWS, s) for s in range(slabs - ROWS)]

    home_of = [
        (f, ((f % 8) * ROWS + (f // 8) % ROWS) * groups + f // (8 * ROWS)) for f in range(slabs * groups)
    ]
    notes = lax.ppermute(notes, both, home_of)
    got = lax.all_to_all(sent, both, 0, 0, axis_index_groups=near, tiled=True)
    got = got.reshape(groups, ROWS, 10, 4, LANES)
    last, first, notes = lax.optimization_barrier((got[:, ROWS - 1], got[:, 0], notes))
    low = lax.ppermute(last, "slab", rise)
    high = lax.ppermute(first, "slab", fall)
    got_m = lax.all_to_all(notes, "slab", 0, 0, axis_index_groups=slab_far, tiled=True)

    analysed = pl.pallas_call(
        functools.partial(analysis_kernel, groups, slabs),
        out_shape=jax.ShapeDtypeStruct((groups, ROWS, 8, 4, LANES), BF16),
        in_specs=[smem] + [vmem] * 4,
        out_specs=vmem,
        scratch_shapes=[
            pltpu.VMEM((80, members, LANES), F32),
            pltpu.VMEM((10, members, LANES), F32),
            pltpu.VMEM((10, members, LANES), F32),
            pltpu.VMEM((72, members, LANES), F32),
            pltpu.VMEM((8, members, 8 * LANES), BF16),
            pltpu.VMEM((8, PAD, 8 * LANES), BF16),
            pltpu.VMEM((2 * members, 8 * PAD), BF16),
            pltpu.VMEM((10, 24, LANES), F32),
        ],
        compiler_params=params,
        name="analysis",
    )(jnp.sqrt(error_precision), got, low, high, got_m)

    home = lax.all_to_all(
        analysed.reshape(blocks, 8, 4, LANES), both, 0, 0, axis_index_groups=near, tiled=True
    )

    return pl.pallas_call(
        unpack_kernel,
        out_shape=jax.ShapeDtypeStruct((4, 2, 4, blocks * LANES), BF16),
        in_specs=[vmem],
        out_specs=vmem,
        compiler_params=params,
        name="unpack",
    )(home)


def solution(mesh):
    return jax.shard_map(
        on_device,
        mesh=mesh,
        in_specs=(
            P("grp", "slab", None, None),
            P("slab", None, None),
            P("slab", None, None),
            P(),
            P("slab"),
            P(None, None, ("slab", "grp")),
            P(),
            P(),
            P(None, ("slab", "grp")),
            P(None, ("slab", "grp")),
        ),
        out_specs=P("grp", "slab", None, None),
        check_vma=False,
    )
```
